256 devices in a mesh: cp: 8 (over z), tp: 8 (over x_lo, y), ep: 4 (over x_hi, core).
Axes of the slice: x: 4 (x_hi: 2, x_lo: 2; x = x_hi * 2 + x_lo), y: 4, z: 8, core: 2. Of those that a mesh axis runs over, the one named last changes fastest.
Arguments:
- layer_input: bfloat16 [8192, 4096], P('cp', ('tp', 'ep')), may hold values from -6 to 6
- output_cot: bfloat16 [8192, 4096], P(('cp', 'tp'), 'ep'), may hold values from -6 to 6
- routes: int32 [8192, 2], P(('cp', 'tp')), may hold values from 0 to 63, all different within a row; in each aligned block of 128 rows (0 to 127, 128 to 255, ...) at most 5 rows name the same one
- gate_values: float32 [8192, 2], P(('cp', 'tp')), may hold values from 0.05 to 1
- gate_weight: bfloat16 [64, 4096, 1536], P(('cp', 'tp'), None, 'ep'), may hold values from -0.09375 to 0.09375
- up_weight: bfloat16 [64, 4096, 1536], P(('cp', 'tp'), None, 'ep'), may hold values from -0.09375 to 0.09375
- down_weight: bfloat16 [64, 1536, 4096], P(('cp', 'tp'), 'ep'), may hold values from -0.15625 to 0.15625
Outputs:
- moe_output: bfloat16 [8192, 4096], P(('cp', 'tp'), 'ep')
- input_grad: bfloat16 [8192, 4096], P(('cp', 'tp'), 'ep')
- gate_grad: float32 [8192, 2], P(('cp', 'tp'))
The draws below stay inside these ranges and needn't reach their ends.
Inputs may be any that keep to these rules, and one draw needn't show every extreme that they name: `routes`: each row names 2 different experts. Within the 128 rows of one device no expert is named by more than 5 rows, a bound that some block reaches.
All inputs are finite; a program needn't handle non-finite values.
Results may differ from the reference program's by a relative error of at most 0.015.
Values may be sent and summed in bfloat16 or wider, within the bound.
No kernel may reach another device: no remote copies, remote signals or barrier semaphores. Data moves between devices by JAX's collectives and lax.ppermute only.
A program may use at most 128 MiB of HBM per device.

```python
import math
import jax
import jax.numpy as jnp
import numpy as np
from jax import lax

D = 4096
FF = 1536
TOP = 2
TOK_DEV = 128
EXPERTS = 64
CAP = 5
TOKENS = 8192
N_EP = 4


def block_scale(rng, shape, cuts, low, high):
    def one(axis_at, shards_of):
        draws = jax.random.uniform(jax.random.fold_in(jax.random.fold_in(rng, 6), axis_at), (shards_of,), jnp.float32, low / len(cuts), high / len(cuts))
        return jnp.repeat(jnp.exp(draws), shape[axis_at] // shards_of).reshape((-1,) + (1,) * (len(shape) - axis_at - 1))

    level = one(*cuts[0])
    for cut in cuts[1:]:
        level = level * one(*cut)
    return level


def shared_out(stream_key, own, number, rows, amount, top, most, lean):
    sequence = jax.random.permutation(stream_key, amount)
    heavy_load, ordinary = load_shares(amount, rows * top, most, lean, True), load_shares(amount, rows * top, most, lean, False)
    places = jnp.arange(amount)

    def named(lengths, offset_by):
        used = int((lengths > 0).sum())
        fixed = max(1, used // 4)
        passed = fixed + (places - fixed + offset_by * (used - fixed)) % max(1, amount - fixed)
        return jnp.zeros((amount,), jnp.int32).at[sequence[jnp.where(places < fixed, places, passed)]].set(jnp.asarray(lengths, jnp.int32))

    lengths = jnp.where(number % 4 == 0, named(heavy_load, number // 4), named(ordinary, number - number // 4 - 1))
    mixed = jax.random.permutation(jax.random.fold_in(own, 3), amount)
    giver, taker = mixed[0:amount // 2 * 2:2], mixed[1:amount // 2 * 2:2]
    slack = jnp.minimum(lengths[giver] - 1, most - lengths[taker]) // 2
    slack = jnp.where((giver == sequence[0]) | (taker == sequence[0]) | (lengths[taker] == 0), 0, jnp.maximum(slack, 0))
    passed = jax.random.randint(jax.random.fold_in(own, 4), (amount // 2,), 0, 1 << 20) % (slack + 1)
    lengths = lengths.at[giver].add(-passed).at[taker].add(passed)
    items = jnp.searchsorted(jnp.cumsum(lengths), jnp.arange(rows * top), side="right").astype(jnp.int32)
    grid = items.reshape(top, rows).T
    grid = grid[jax.random.permutation(jax.random.fold_in(own, 1), rows)]
    offset_by = jax.random.randint(jax.random.fold_in(own, 2), (rows, 1), 0, top)
    return jnp.take_along_axis(grid, (jnp.arange(top)[None, :] + offset_by) % top, axis=1)


def load_shares(amount, total, reach, slope, full):
    portions = [(1 << 20) // math.isqrt(grade ** slope) + 1 for grade in range(1, amount + 1)]
    largest = reach if full else min(reach, max(-(-total // amount), total * portions[0] // sum(portions)))
    least = 1 if total - largest >= amount - 1 else 0
    counts, rest = [largest] + [least] * (amount - 1), total - largest - least * (amount - 1)
    while rest > 0:
        candidates = [i for i in range(1, amount) if counts[i] < largest] or [i for i in range(1, amount) if counts[i] < reach]
        mass, budget = sum([portions[i] for i in candidates]), rest
        for i in candidates:
            extra = min(reach - counts[i], max(1, budget * portions[i] // mass), rest)
            counts[i] = counts[i] + extra
            rest = rest - extra
    return np.array(counts)


def noise(key, extent, deviation, reach, shards=(), kind=jnp.bfloat16):
    values = jax.random.normal(key, extent, jnp.float32) * deviation
    if len(shards) > 0:
        values = block_scale(key, extent, shards, -0.22, 0.18) * values
    return jnp.clip(values, min=-reach, max=reach).astype(kind)


def setup_inputs(seed: int = 0) -> dict:
    arg_keys = jax.random.split(jax.random.key(seed), 8)
    layer_input = noise(arg_keys[0], (TOKENS, D), 1.0, 6.0, ((0, 8), (1, 32)))
    output_cot = noise(arg_keys[1], (TOKENS, D), 1.0, 6.0, ((0, 64), (1, 4)))
    routes_keys = jax.random.split(jax.random.fold_in(arg_keys[2], 1), TOKENS // TOK_DEV)
    routes_turns = jax.random.permutation(jax.random.fold_in(arg_keys[2], 3), TOKENS // TOK_DEV)
    routes = jax.vmap(lambda own, number: shared_out(jax.random.fold_in(arg_keys[2], 2), own, number, TOK_DEV, EXPERTS, TOP, CAP, 2))(routes_keys, routes_turns).reshape((TOKENS, TOP))
    gate_values = jnp.clip(jnp.exp(math.log(1.0) - 2.9957323 * jax.random.uniform(arg_keys[3], (TOKENS, TOP), jnp.float32) ** block_scale(arg_keys[3], (TOKENS, TOP), ((0, 64),), -0.2, 0.2)), 0.05, 1.0)
    gate_weight = noise(arg_keys[4], (EXPERTS, D, FF), D ** -0.5, 0.09375, ((0, 64), (2, 4)))
    up_weight = noise(arg_keys[5], (EXPERTS, D, FF), D ** -0.5, 0.09375, ((0, 64), (2, 4)))
    down_weight = noise(arg_keys[6], (EXPERTS, FF, D), FF ** -0.5, 0.15625, ((0, 64), (1, 4)))
    return {"layer_input": layer_input, "output_cot": output_cot, "routes": routes, "gate_values": gate_values, "gate_weight": gate_weight, "up_weight": up_weight, "down_weight": down_weight}


def transposed(left, right):
    return lax.dot_general(left, right, (((1,), (1,)), ((), ())), preferred_element_type=jnp.float32)


def reference(layer_input, output_cot, routes, gate_values, gate_weight, up_weight, down_weight):
    flat_routes = routes.reshape(-1).astype(jnp.int32)
    entries = flat_routes.shape[0]
    flat_gates = gate_values.reshape(-1)
    slot_total = EXPERTS * CAP
    unit_width = FF // N_EP
    entry_order = jnp.arange(entries, dtype=jnp.int32)

    def one_expert(carried, inputs):
        acc_out, acc_grad = carried
        expert, gate_w, up_w, down_w = inputs
        chosen = flat_routes == expert
        sort_key = jnp.where(chosen, 0, entries).astype(jnp.int32) + entry_order
        members = jnp.argsort(sort_key)[:slot_total].astype(jnp.int32)
        is_live = chosen[members][:, None]
        token_of = members // TOP
        member_rows = layer_input[token_of]
        cot_rows = (flat_gates[members][:, None] * output_cot[token_of].astype(jnp.float32)).astype(jnp.bfloat16)
        pre_gate = jnp.dot(member_rows, gate_w, preferred_element_type=jnp.float32)
        pre_up = jnp.dot(member_rows, up_w, preferred_element_type=jnp.float32)
        sigmoid_gate = jax.nn.sigmoid(pre_gate)
        silu_gate = pre_gate * sigmoid_gate
        act = (silu_gate * pre_up).astype(jnp.bfloat16)
        d_act = transposed(cot_rows, down_w)
        d_gate = (d_act * pre_up * sigmoid_gate * (1.0 + pre_gate * (1.0 - sigmoid_gate))).astype(jnp.bfloat16)
        d_up = (d_act * silu_gate).astype(jnp.bfloat16)
        expert_out = jnp.zeros((slot_total, D), jnp.float32)
        grad_rows = jnp.zeros((slot_total, D), jnp.float32)
        for block in range(N_EP):
            low = block * unit_width
            high = low + unit_width
            part = jnp.dot(act[:, low:high], down_w[low:high], preferred_element_type=jnp.float32).astype(jnp.bfloat16)
            expert_out = expert_out + part.astype(jnp.float32)
            grad_part = transposed(d_gate[:, low:high], gate_w[:, low:high]) + transposed(d_up[:, low:high], up_w[:, low:high])
            grad_rows = grad_rows + grad_part.astype(jnp.bfloat16).astype(jnp.float32)
        acc_out = acc_out.at[members].add(jnp.where(is_live, expert_out, 0.0))
        acc_grad = acc_grad.at[members].add(jnp.where(is_live, grad_rows, 0.0))
        return (acc_out, acc_grad), None

    start = (jnp.zeros((entries, D), jnp.float32), jnp.zeros((entries, D), jnp.float32))
    (acc_out, acc_grad), _ = lax.scan(one_expert, start, (jnp.arange(EXPERTS, dtype=jnp.int32), gate_weight, up_weight, down_weight))
    picked = acc_out.reshape(TOKENS, TOP, D)
    moe_output = jnp.sum(gate_values[:, :, None] * picked, axis=1).astype(jnp.bfloat16)
    input_grad = jnp.sum(acc_grad.reshape(TOKENS, TOP, D), axis=1).astype(jnp.bfloat16)
    gate_grad = jnp.sum(output_cot.astype(jnp.float32)[:, None, :] * picked, axis=-1)
    return moe_output, input_grad, gate_grad
```

```python
import functools

import jax
import jax.numpy as jnp
from jax import lax
from jax.experimental import pallas as pl
from jax.experimental.pallas import tpu as pltpu
from jax.sharding import PartitionSpec as P

BF = jnp.bfloat16
F32 = jnp.float32
LANES = 128


def nt(left, right):
    return lax.dot_general(
        left, right, (((1,), (1,)), ((), ())), preferred_element_type=F32
    )


def tn(left, right):
    return lax.dot_general(
        left, right, (((0,), (0,)), ((), ())), preferred_element_type=F32
    )


def slot_masks(routes, experts, capacity):
    picks, tokens = routes.shape
    expert = lax.broadcasted_iota(jnp.int32, (experts, tokens), 0)
    earlier = (
        lax.broadcasted_iota(jnp.int32, (tokens, tokens), 0)
        < lax.broadcasted_iota(jnp.int32, (tokens, tokens), 1)
    ).astype(F32).astype(BF)
    slot = lax.broadcasted_iota(jnp.int32, (experts * capacity, tokens), 0)
    taken = jnp.zeros((experts, 1), F32)
    masks = []
    for k in range(picks):
        named = routes[k : k + 1, :]
        chosen = (expert == named).astype(F32)
        before = jnp.dot(chosen.astype(BF), earlier, preferred_element_type=F32) + taken
        rank = jnp.sum(before * chosen, axis=0, keepdims=True)
        place = named * capacity + rank.astype(jnp.int32)
        masks.append((slot == place).astype(F32))
        taken = taken + jnp.sum(chosen, axis=1, keepdims=True)
    return masks


def tile_rows(values, blocks, wide_ref, out_ref):
    rows = wide_ref.shape[0] // blocks
    for f in range(blocks):
        wide_ref[pl.ds(f, rows, stride=blocks), :] = values(f)
    out_ref[...] = wide_ref[...].astype(BF)


def untile_rows(in_ref, blocks, wide_ref, out_ref):
    rows = wide_ref.shape[0] // blocks
    wide_ref[...] = in_ref[...].astype(F32)
    for f in range(blocks):
        out_ref[:, f * LANES : (f + 1) * LANES] = wide_ref[
            pl.ds(f, rows, stride=blocks), :
        ].astype(BF)


def pack_cot_kernel(experts, capacity, routes_ref, gates_ref, cot_ref, out_ref, wide_ref):
    masks = slot_masks(routes_ref[...], experts, capacity)
    both = functools.reduce(lambda a, b: a + b, masks)
    gate = functools.reduce(
        lambda a, b: a + b,
        [
            jnp.sum(m * gates_ref[k : k + 1, :], axis=1, keepdims=True)
            for k, m in enumerate(masks)
        ],
    )
    both = both.astype(BF)
    blocks = cot_ref.shape[1] // LANES

    def block(f):
        rows = jnp.dot(
            both, cot_ref[:, f * LANES : (f + 1) * LANES], preferred_element_type=F32
        )
        return rows * gate

    tile_rows(block, blocks, wide_ref, out_ref)


def pack_input_kernel(experts, capacity, routes_ref, x_ref, out_ref, wide_ref):
    masks = slot_masks(routes_ref[...], experts, capacity)
    both = functools.reduce(lambda a, b: a + b, masks).astype(BF)
    blocks = x_ref.shape[0]
    tile_rows(
        lambda f: jnp.dot(both, x_ref[f], preferred_element_type=F32),
        blocks,
        wide_ref,
        out_ref,
    )


def dact_kernel(ep_ref, c0, c1, c2, c3, down_hbm, out_ref, wide, lhs, weights, sems):
    ep = ep_ref[0]
    quarter = lhs.shape[1]
    copies = []
    for j in range(4):
        start = pl.multiple_of((ep ^ j) * quarter, LANES)
        copy = pltpu.make_async_copy(
            down_hbm.at[:, pl.ds(start, quarter)], weights.at[j], sems.at[j]
        )
        copy.start()
        copies.append(copy)
    for j, part in enumerate((c0, c1, c2, c3)):
        untile_rows(part, quarter // LANES, wide, lhs)
        copies[j].wait()
        product = nt(lhs[...], weights[j])
        if j == 0:
            out_ref[...] = product
        else:
            out_ref[...] += product


def pre_kernel(ep_ref, x0, x1, gate_hbm, up_hbm, g_ref, u_ref, wide, lhs, weights, sems):
    ep = ep_ref[0]
    width = lhs.shape[1]
    copies = []
    for j in range(2):
        for i, w in enumerate((gate_hbm, up_hbm)):
            copy = pltpu.make_async_copy(
                w.at[:, ep ^ j], weights.at[2 * j + i], sems.at[2 * j + i]
            )
            copy.start()
            copies.append(copy)
    for j, part in enumerate((x0, x1)):
        untile_rows(part, width // LANES, wide, lhs)
        for i, ref in enumerate((g_ref, u_ref)):
            copies[2 * j + i].wait()
            w = weights[2 * j + i].reshape(width, -1)
            product = jnp.dot(lhs[...], w, preferred_element_type=F32)
            if j == 0:
                ref[...] = product
            else:
                ref[...] += product


def forward_kernel(
    ep_ref, x2, x3, g_in, u_in, gate_hbm, up_hbm, down_hbm,
    act_ref, silu_ref, dsilu_ref, send_ref, keep_ref,
    wide, lhs, g_acc, u_acc, weights, down, sems,
):
    ep = ep_ref[0]
    width = lhs.shape[1]
    copies = []
    for j in range(2):
        for i, w in enumerate((gate_hbm, up_hbm)):
            copy = pltpu.make_async_copy(
                w.at[:, ep ^ (j + 2)], weights.at[2 * j + i], sems.at[2 * j + i]
            )
            copy.start()
            copies.append(copy)
    for j, q in enumerate((ep ^ 3, ep ^ 2)):
        start = pl.multiple_of(q * width, LANES)
        copy = pltpu.make_async_copy(
            down_hbm.at[:, pl.ds(start, width)], down.at[j], sems.at[4 + j]
        )
        copy.start()
        copies.append(copy)
    for j, part in enumerate((x2, x3)):
        untile_rows(part, width // LANES, wide, lhs)
        for i, (acc, old) in enumerate(((g_acc, g_in), (u_acc, u_in))):
            copies[2 * j + i].wait()
            w = weights[2 * j + i].reshape(width, -1)
            product = jnp.dot(lhs[...], w, preferred_element_type=F32)
            if j == 0:
                acc[...] = old[...] + product
            else:
                acc[...] += product
    pre_gate = g_acc[...]
    pre_up = u_acc[...]
    sigmoid = jax.nn.sigmoid(pre_gate)
    silu = pre_gate * sigmoid
    silu_ref[...] = silu
    dsilu_ref[...] = pre_up * sigmoid * (1.0 + pre_gate * (1.0 - sigmoid))
    act_ref[...] = (silu * pre_up).astype(BF)
    copies[4].wait()
    send_ref[...] = jnp.dot(act_ref[...], down[0], preferred_element_type=F32).astype(BF)
    copies[5].wait()
    keep_ref[...] = jnp.dot(act_ref[...], down[1], preferred_element_type=F32)


def own_out_kernel(ep_ref, act_ref, down_hbm, send_ref, keep_ref, down, sems):
    ep = ep_ref[0]
    width = send_ref.shape[1]
    copies = []
    for j, q in enumerate((ep ^ 1, ep)):
        start = pl.multiple_of(q * width, LANES)
        copy = pltpu.make_async_copy(
            down_hbm.at[:, pl.ds(start, width)], down.at[j], sems.at[j]
        )
        copy.start()
        copies.append(copy)
    copies[0].wait()
    send_ref[...] = jnp.dot(act_ref[...], down[0], preferred_element_type=F32).astype(BF)
    copies[1].wait()
    keep_ref[...] = jnp.dot(act_ref[...], down[1], preferred_element_type=F32)


def grad_kernel(
    ep_ref, dact_ref, silu_ref, dsilu_ref, gate_hbm, up_hbm,
    dgate_ref, dup_ref, send_ref, keep_ref, weights, sems,
):
    ep = ep_ref[0]
    width = send_ref.shape[1]
    copies = []
    for j, q in enumerate((ep ^ 3, ep ^ 2)):
        for i, w in enumerate((gate_hbm, up_hbm)):
            copy = pltpu.make_async_copy(w.at[q], weights.at[2 * j + i], sems.at[2 * j + i])
            copy.start()
            copies.append(copy)
    d_act = dact_ref[...]
    dgate_ref[...] = (d_act * dsilu_ref[...]).astype(BF)
    dup_ref[...] = (d_act * silu_ref[...]).astype(BF)
    copies[0].wait()
    copies[1].wait()
    send_ref[...] = (nt(dgate_ref[...], weights[0]) + nt(dup_ref[...], weights[1])).astype(BF)
    copies[2].wait()
    copies[3].wait()
    keep_ref[...] = nt(dgate_ref[...], weights[2]) + nt(dup_ref[...], weights[3])


def own_grad_kernel(
    ep_ref, dgate_ref, dup_ref, gate_hbm, up_hbm, send_ref, keep_ref, weights, sems
):
    ep = ep_ref[0]
    copies = []
    for j, q in enumerate((ep ^ 1, ep)):
        for i, w in enumerate((gate_hbm, up_hbm)):
            copy = pltpu.make_async_copy(w.at[q], weights.at[2 * j + i], sems.at[2 * j + i])
            copy.start()
            copies.append(copy)
    copies[0].wait()
    copies[1].wait()
    send_ref[...] = (nt(dgate_ref[...], weights[0]) + nt(dup_ref[...], weights[1])).astype(BF)
    copies[2].wait()
    copies[3].wait()
    keep_ref[...] = nt(dgate_ref[...], weights[2]) + nt(dup_ref[...], weights[3])


def chip_sum_kernel(keep_ref, came_ref, out_ref):
    out_ref[...] = (keep_ref[...] + came_ref[...].astype(F32)).astype(BF)


def finish_kernel(keep_ref, near_ref, far_ref, out_ref, wide_ref):
    def block(f):
        cols = slice(f * LANES, (f + 1) * LANES)
        return keep_ref[:, cols] + near_ref[:, cols].astype(F32) + far_ref[:, cols].astype(F32)

    tile_rows(block, keep_ref.shape[1] // LANES, wide_ref, out_ref)


def combine_out_kernel(
    experts, capacity, routes_ref, gates_ref, cot_ref, rows_ref, out_ref, grad_ref, wide, lhs
):
    masks = slot_masks(routes_ref[...], experts, capacity)
    untile_rows(rows_ref, lhs.shape[1] // LANES, wide, lhs)
    cot = cot_ref[...].astype(F32)
    total = None
    grads = []
    for k, m in enumerate(masks):
        picked = tn(m.astype(BF), lhs[...])
        term = gates_ref[:, k : k + 1] * picked
        total = term if total is None else total + term
        grads.append(jnp.sum(cot * picked, axis=1, keepdims=True))
    out_ref[...] = total.astype(BF)
    grad_ref[...] = jnp.concatenate(grads, axis=1)


def combine_grad_kernel(experts, capacity, routes_ref, rows_ref, out_ref, wide, lhs):
    masks = slot_masks(routes_ref[...], experts, capacity)
    both = functools.reduce(lambda a, b: a + b, masks).astype(BF)
    untile_rows(rows_ref, lhs.shape[1] // LANES, wide, lhs)
    out_ref[...] = tn(both, lhs[...]).astype(BF)


SMEM = pl.BlockSpec(memory_space=pltpu.SMEM)
VMEM = pl.BlockSpec(memory_space=pltpu.VMEM)
ANY = pl.BlockSpec(memory_space=pl.ANY)


def call(kernel, specs, outs, scratch, flops, moved, *operands):
    single = not isinstance(outs, (list, tuple))
    return pl.pallas_call(
        kernel,
        out_shape=outs,
        in_specs=specs,
        out_specs=VMEM if single else [VMEM] * len(outs),
        scratch_shapes=scratch,
        compiler_params=pltpu.CompilerParams(vmem_limit_bytes=40 * 1024 * 1024),
        cost_estimate=pl.CostEstimate(flops=flops, bytes_accessed=moved, transcendentals=0),
    )(*operands)


def local(layer_input, output_cot, routes, gate_values, gate_weight, up_weight, down_weight):
    tokens, picks = routes.shape
    experts = lax.axis_size(("cp", "tp"))
    tp = lax.axis_size("tp")
    ep_size = lax.axis_size("ep")
    capacity = max(2, tokens * picks * 5 // (4 * experts))
    slots = experts * capacity
    width = output_cot.shape[1]
    blocks = width // LANES
    hidden = gate_weight.shape[2]
    tiled = slots * blocks
    ep = lax.axis_index("ep").astype(jnp.int32).reshape(1)
    routes_t = routes.T
    gates_t = gate_values.T
    down_w = down_weight[0]
    gate_x = gate_weight.reshape(tp, ep_size, LANES, hidden)
    up_x = up_weight.reshape(tp, ep_size, LANES, hidden)
    gate_q = gate_weight.reshape(ep_size, width, hidden)
    up_q = up_weight.reshape(ep_size, width, hidden)
    shape = jax.ShapeDtypeStruct
    wide = pltpu.VMEM((tiled, LANES), F32)
    lhs = pltpu.VMEM((slots, width), BF)
    near = [(i, i ^ 1) for i in range(ep_size)]
    far = [(i, i ^ 2) for i in range(ep_size)]

    def exchange(rows):
        return lax.all_to_all(
            rows.reshape(experts, capacity * blocks, LANES),
            ("cp", "tp"),
            split_axis=0,
            concat_axis=0,
            tiled=True,
        ).reshape(tiled, LANES)

    def gather(own):
        across = lax.ppermute(own, "ep", far)
        beside = lax.ppermute(own, "ep", near)
        return own, beside, across, lax.ppermute(across, "ep", near)

    x_cols = lax.all_to_all(
        layer_input.reshape(tp, tokens, LANES), "tp", split_axis=0, concat_axis=0, tiled=True
    )
    moved = slots * width * 6
    cot_rows = call(
        functools.partial(pack_cot_kernel, experts, capacity),
        [VMEM] * 3, shape((tiled, LANES), BF), [wide], 10**8, moved,
        routes_t, gates_t, output_cot,
    )
    c0, c1, c2, c3 = gather(exchange(cot_rows))
    x_rows = call(
        functools.partial(pack_input_kernel, experts, capacity),
        [VMEM] * 2, shape((tiled, LANES), BF), [wide], 10**8, moved,
        routes_t, x_cols,
    )
    x0, x1, x2, x3 = gather(exchange(x_rows))

    sems = lambda n: pltpu.SemaphoreType.DMA((n,))
    acc = shape((slots, hidden), F32)
    dot_flops = 2 * slots * width * hidden
    d_act = call(
        dact_kernel, [SMEM] + [VMEM] * 4 + [ANY], acc,
        [wide, lhs, pltpu.VMEM((4, hidden, width), BF), sems(4)],
        4 * dot_flops, 2 * moved, ep, c0, c1, c2, c3, down_w,
    )
    weights_x = pltpu.VMEM((4, tp, LANES, hidden), BF)
    weights_q = pltpu.VMEM((4, width, hidden), BF)
    down_half = pltpu.VMEM((2, hidden, width), BF)
    g_part, u_part = call(
        pre_kernel, [SMEM] + [VMEM] * 2 + [ANY] * 2, [acc, acc],
        [wide, lhs, weights_x, sems(4)],
        4 * dot_flops, 2 * moved, ep, x0, x1, gate_x, up_x,
    )
    send_t = shape((slots, width), BF)
    keep_t = shape((slots, width), F32)
    hid = shape((slots, hidden), BF)
    act, silu, dsilu, out_send, out_keep = call(
        forward_kernel, [SMEM] + [VMEM] * 4 + [ANY] * 3, [hid, acc, acc, send_t, keep_t],
        [wide, lhs, pltpu.VMEM((slots, hidden), F32), pltpu.VMEM((slots, hidden), F32),
         weights_x, down_half, sems(6)],
        6 * dot_flops, 3 * moved, ep, x2, x3, g_part, u_part, gate_x, up_x, down_w,
    )
    out_far = call(
        chip_sum_kernel, [VMEM] * 2, send_t, [], 10**6, moved,
        out_keep, lax.ppermute(out_send, "ep", near),
    )
    out_far = lax.ppermute(out_far, "ep", far)
    out_send2, out_keep2 = call(
        own_out_kernel, [SMEM, VMEM, ANY], [send_t, keep_t], [down_half, sems(2)],
        2 * dot_flops, 2 * moved, ep, act, down_w,
    )
    out_near = lax.ppermute(out_send2, "ep", near)
    d_gate, d_up, grad_send, grad_keep = call(
        grad_kernel, [SMEM] + [VMEM] * 3 + [ANY] * 2, [hid, hid, send_t, keep_t],
        [weights_q, sems(4)],
        4 * dot_flops, 3 * moved, ep, d_act, silu, dsilu, gate_q, up_q,
    )
    grad_far = call(
        chip_sum_kernel, [VMEM] * 2, send_t, [], 10**6, moved,
        grad_keep, lax.ppermute(grad_send, "ep", near),
    )
    grad_far = lax.ppermute(grad_far, "ep", far)
    grad_send2, grad_keep2 = call(
        own_grad_kernel, [SMEM] + [VMEM] * 2 + [ANY] * 2, [send_t, keep_t],
        [weights_q, sems(4)],
        4 * dot_flops, 3 * moved, ep, d_gate, d_up, gate_q, up_q,
    )
    grad_near = lax.ppermute(grad_send2, "ep", near)
    out_rows = call(
        finish_kernel, [VMEM] * 3, shape((tiled, LANES), BF), [wide], 10**6, moved,
        out_keep2, out_near, out_far,
    )
    out_back = exchange(out_rows)
    grad_rows = call(
        finish_kernel, [VMEM] * 3, shape((tiled, LANES), BF), [wide], 10**6, moved,
        grad_keep2, grad_near, grad_far,
    )
    grad_back = exchange(grad_rows)
    moe_output, gate_grad = call(
        functools.partial(combine_out_kernel, experts, capacity), [VMEM] * 4,
        [shape((tokens, width), BF), shape((tokens, picks), F32)], [wide, lhs], 10**8, moved,
        routes_t, gate_values, output_cot, out_back,
    )
    gate_grad = gate_grad + lax.ppermute(gate_grad, "ep", near)
    gate_grad = gate_grad + lax.ppermute(gate_grad, "ep", far)
    input_grad = call(
        functools.partial(combine_grad_kernel, experts, capacity), [VMEM] * 2,
        shape((tokens, width), BF), [wide, lhs], 10**8, moved,
        routes_t, grad_back,
    )
    return (moe_output, input_grad, gate_grad)


def solution(mesh):
    placed = (
        P("cp", ("tp", "ep")),
        P(("cp", "tp"), "ep"),
        P(("cp", "tp"), None),
        P(("cp", "tp"), None),
        P(("cp", "tp"), None, "ep"),
        P(("cp", "tp"), None, "ep"),
        P(("cp", "tp"), "ep", None),
    )
    return jax.shard_map(
        local,
        mesh=mesh,
        in_specs=placed,
        out_specs=(P(("cp", "tp"), "ep"), P(("cp", "tp"), "ep"), P(("cp", "tp"), None)),
        check_vma=False,
    )
```

```python
import functools

import jax
import jax.numpy as jnp
from jax import lax
from jax.experimental import pallas as pl
from jax.experimental.pallas import tpu as pltpu
from jax.sharding import PartitionSpec as P

BF = jnp.bfloat16
F32 = jnp.float32
LANES = 128
VMEM_BYTES = 24 * 1024 * 1024
LONG = 2 * 10**11


def nt(left, right):
    return lax.dot_general(
        left, right, (((1,), (1,)), ((), ())), preferred_element_type=F32
    )


def tn(left, right):
    return lax.dot_general(
        left, right, (((0,), (0,)), ((), ())), preferred_element_type=F32
    )


def slot_masks(routes, experts, capacity):
    picks, tokens = routes.shape
    expert = lax.broadcasted_iota(jnp.int32, (experts, tokens), 0)
    earlier = (
        lax.broadcasted_iota(jnp.int32, (tokens, tokens), 0)
        < lax.broadcasted_iota(jnp.int32, (tokens, tokens), 1)
    ).astype(F32).astype(BF)
    slot = lax.broadcasted_iota(jnp.int32, (experts * capacity, tokens), 0)
    taken = jnp.zeros((experts, 1), F32)
    masks = []
    for k in range(picks):
        named = routes[k : k + 1, :]
        chosen = (expert == named).astype(F32)
        before = jnp.dot(chosen.astype(BF), earlier, preferred_element_type=F32) + taken
        rank = jnp.sum(before * chosen, axis=0, keepdims=True)
        place = named * capacity + rank.astype(jnp.int32)
        masks.append((slot == place).astype(F32))
        taken = taken + jnp.sum(chosen, axis=1, keepdims=True)
    return masks


def tile_rows(values, blocks, wide_ref, out_ref):
    rows = wide_ref.shape[0] // blocks
    for f in range(blocks):
        wide_ref[pl.ds(f, rows, stride=blocks), :] = values(f)
    out_ref[...] = wide_ref[...].astype(BF)


def untile_rows(in_ref, blocks, wide_ref, out_ref):
    rows = wide_ref.shape[0] // blocks
    wide_ref[...] = in_ref[...].astype(F32)
    for f in range(blocks):
        out_ref[:, f * LANES : (f + 1) * LANES] = wide_ref[
            pl.ds(f, rows, stride=blocks), :
        ].astype(BF)


def pack_cot_kernel(
    experts, capacity, routes_ref, gates_ref, cot_ref, out_ref, wide_ref
):
    masks = slot_masks(routes_ref[...], experts, capacity)
    both = functools.reduce(lambda a, b: a + b, masks)
    gate = functools.reduce(
        lambda a, b: a + b,
        [
            jnp.sum(m * gates_ref[k : k + 1, :], axis=1, keepdims=True)
            for k, m in enumerate(masks)
        ],
    )
    both = both.astype(BF)
    blocks = cot_ref.shape[1] // LANES

    def block(f):
        rows = jnp.dot(
            both, cot_ref[:, f * LANES : (f + 1) * LANES], preferred_element_type=F32
        )
        return rows * gate

    tile_rows(block, blocks, wide_ref, out_ref.at[0])
    out_ref[1] = out_ref[0]


def pack_input_kernel(experts, capacity, routes_ref, x_ref, after, out_ref, wide_ref):
    masks = slot_masks(routes_ref[...], experts, capacity)
    both = functools.reduce(lambda a, b: a + b, masks).astype(BF)
    blocks = x_ref.shape[0]
    tile_rows(
        lambda f: jnp.dot(both, x_ref[f], preferred_element_type=F32),
        blocks,
        wide_ref,
        out_ref,
    )


def tie_kernel(x_ref, *rest):
    pass


class Loads:
    def __init__(self, refs, buffer, sems):
        self.buffer = buffer
        self.copies = [
            pltpu.make_async_copy(ref, buffer.at[i], sems.at[i]) for i, ref in enumerate(refs)
        ]
        for copy in self.copies:
            copy.start()

    def __getitem__(self, i):
        self.copies[i].wait()
        block = self.buffer[i]
        return block.reshape(-1, block.shape[-1])


def columns(ref, index, width):
    return ref.at[:, pl.ds(pl.multiple_of(index * width, LANES), width)]


def dact_first_kernel(place_ref, c, down, out_ref, wide, lhs, buffer, sems):
    core = place_ref[0] & 1
    width = lhs.shape[1]
    w = Loads([columns(down, core + 2 * j, width) for j in range(2)], buffer, sems)
    untile_rows(c.at[0], width // LANES, wide, lhs)
    out_ref[...] = nt(lhs[...], w[0])
    untile_rows(c.at[1], width // LANES, wide, lhs)
    out_ref[...] += nt(lhs[...], w[1])


def dact_last_kernel(place_ref, c, part, down, out_ref, wide, lhs, buffer, sems):
    core = 1 - (place_ref[0] & 1)
    width = lhs.shape[1]
    w = Loads([columns(down, core + 2 * j, width) for j in range(2)], buffer, sems)
    untile_rows(c.at[0], width // LANES, wide, lhs)
    out_ref[...] = part[...] + nt(lhs[...], w[0])
    untile_rows(c.at[1], width // LANES, wide, lhs)
    out_ref[...] += nt(lhs[...], w[1])


def pre_first_kernel(place_ref, x0, x1, gate, up, g_ref, u_ref, wide, lhs, buffer, sems):
    ep = place_ref[0]
    w = Loads([gate.at[:, ep], up.at[:, ep], gate.at[:, ep ^ 1], up.at[:, ep ^ 1]], buffer, sems)
    blocks = lhs.shape[1] // LANES
    untile_rows(x0, blocks, wide, lhs)
    g_ref[...] = jnp.dot(lhs[...], w[0], preferred_element_type=F32)
    u_ref[...] = jnp.dot(lhs[...], w[1], preferred_element_type=F32)
    untile_rows(x1, blocks, wide, lhs)
    g_ref[...] += jnp.dot(lhs[...], w[2], preferred_element_type=F32)
    u_ref[...] += jnp.dot(lhs[...], w[3], preferred_element_type=F32)


def pre_next_kernel(place_ref, x2, g_in, u_in, gate, up, g_ref, u_ref, wide, lhs, buffer, sems):
    ep = place_ref[0]
    w = Loads([gate.at[:, ep ^ 2], up.at[:, ep ^ 2]], buffer, sems)
    untile_rows(x2, lhs.shape[1] // LANES, wide, lhs)
    g_ref[...] = g_in[...] + jnp.dot(lhs[...], w[0], preferred_element_type=F32)
    u_ref[...] = u_in[...] + jnp.dot(lhs[...], w[1], preferred_element_type=F32)


def forward_kernel(
    place_ref, x3, g_in, u_in, gate, up, down,
    act_ref, silu_ref, dsilu_ref, send_ref, wide, lhs, buffer, down_buffer, sems, down_sems,
):
    ep = place_ref[0]
    width = lhs.shape[1]
    w = Loads([gate.at[:, ep ^ 3], up.at[:, ep ^ 3]], buffer, sems)
    w_down = Loads([columns(down, ep ^ 3, width)], down_buffer, down_sems)
    untile_rows(x3, width // LANES, wide, lhs)
    pre_gate = g_in[...] + jnp.dot(lhs[...], w[0], preferred_element_type=F32)
    pre_up = u_in[...] + jnp.dot(lhs[...], w[1], preferred_element_type=F32)
    sigmoid = jax.nn.sigmoid(pre_gate)
    silu = pre_gate * sigmoid
    silu_ref[...] = silu
    dsilu_ref[...] = pre_up * sigmoid * (1.0 + pre_gate * (1.0 - sigmoid))
    act_ref[...] = (silu * pre_up).astype(BF)
    send_ref[...] = jnp.dot(act_ref[...], w_down[0], preferred_element_type=F32).astype(BF)


def keep_kernel(place_ref, act_ref, down, keep_ref, buffer, sems):
    w = Loads([columns(down, place_ref[0] ^ 2, keep_ref.shape[1])], buffer, sems)
    keep_ref[...] = jnp.dot(act_ref[...], w[0], preferred_element_type=F32)


def grad_kernel(
    place_ref, dact_ref, silu_ref, dsilu_ref, gate, up,
    dgate_ref, dup_ref, send_ref, keep_ref, buffer, sems,
):
    ep = place_ref[0]
    w = Loads([gate.at[ep ^ 3], up.at[ep ^ 3], gate.at[ep ^ 2], up.at[ep ^ 2]], buffer, sems)
    d_act = dact_ref[...]
    dgate_ref[...] = (d_act * dsilu_ref[...]).astype(BF)
    dup_ref[...] = (d_act * silu_ref[...]).astype(BF)
    send_ref[...] = (nt(dgate_ref[...], w[0]) + nt(dup_ref[...], w[1])).astype(BF)
    keep_ref[...] = nt(dgate_ref[...], w[2]) + nt(dup_ref[...], w[3])


def own_out_kernel(place_ref, act_ref, down, send_ref, keep_ref, buffer, sems):
    ep = place_ref[0]
    width = send_ref.shape[1]
    w = Loads([columns(down, ep ^ 1, width), columns(down, ep, width)], buffer, sems)
    send_ref[...] = jnp.dot(act_ref[...], w[0], preferred_element_type=F32).astype(BF)
    keep_ref[...] = jnp.dot(act_ref[...], w[1], preferred_element_type=F32)


def own_grad_kernel(place_ref, dgate_ref, dup_ref, gate, up, send_ref, keep_ref, buffer, sems):
    ep = place_ref[0]
    w = Loads([gate.at[ep ^ 1], up.at[ep ^ 1], gate.at[ep], up.at[ep]], buffer, sems)
    send_ref[...] = (nt(dgate_ref[...], w[0]) + nt(dup_ref[...], w[1])).astype(BF)
    keep_ref[...] = nt(dgate_ref[...], w[2]) + nt(dup_ref[...], w[3])


def chip_sum_kernel(keep_ref, came_ref, after, out_ref):
    out_ref[...] = (keep_ref[...] + came_ref[...].astype(F32)).astype(BF)


def finish_kernel(keep_ref, near_ref, far_ref, after, out_ref, wide_ref):
    def block(f):
        cols = slice(f * LANES, (f + 1) * LANES)
        return keep_ref[:, cols] + near_ref[:, cols].astype(F32) + far_ref[:, cols].astype(F32)

    tile_rows(block, keep_ref.shape[1] // LANES, wide_ref, out_ref)


def combine_out_kernel(
    experts, capacity, routes_ref, gates_ref, cot_ref, rows_ref, out_ref, grad_ref, wide, lhs
):
    masks = slot_masks(routes_ref[...], experts, capacity)
    untile_rows(rows_ref, lhs.shape[1] // LANES, wide, lhs)
    cot = cot_ref[...].astype(F32)
    total = None
    grads = []
    for k, m in enumerate(masks):
        picked = tn(m.astype(BF), lhs[...])
        term = gates_ref[:, k : k + 1] * picked
        total = term if total is None else total + term
        grads.append(jnp.sum(cot * picked, axis=1, keepdims=True))
    out_ref[...] = total.astype(BF)
    grad_ref[...] = jnp.concatenate(grads, axis=1)


def combine_grad_kernel(experts, capacity, routes_ref, rows_ref, out_ref, wide, lhs):
    masks = slot_masks(routes_ref[...], experts, capacity)
    both = functools.reduce(lambda a, b: a + b, masks).astype(BF)
    untile_rows(rows_ref, lhs.shape[1] // LANES, wide, lhs)
    out_ref[...] = tn(both, lhs[...]).astype(BF)


SMEM = pl.BlockSpec(memory_space=pltpu.SMEM)
VMEM = pl.BlockSpec(memory_space=pltpu.VMEM)
ANY = pl.BlockSpec(memory_space=pl.ANY)
HBM = pl.BlockSpec(memory_space=pltpu.HBM)


def call(kernel, specs, outs, scratch, flops, moved, *operands):
    single = not isinstance(outs, (list, tuple))
    return pl.pallas_call(
        kernel,
        out_shape=outs,
        in_specs=specs,
        out_specs=VMEM if single else [VMEM] * len(outs),
        scratch_shapes=scratch,
        compiler_params=pltpu.CompilerParams(vmem_limit_bytes=VMEM_BYTES),
        cost_estimate=pl.CostEstimate(flops=flops, bytes_accessed=moved, transcendentals=0),
    )(*operands)


def tie(x, *after):
    return pl.pallas_call(
        tie_kernel,
        out_shape=jax.ShapeDtypeStruct(x.shape, x.dtype),
        in_specs=[ANY] * (1 + len(after)),
        out_specs=ANY,
        input_output_aliases={0: 0},
    )(x, *after)


def local(layer_input, output_cot, routes, gate_values, gate_weight, up_weight, down_weight):
    tokens, picks = routes.shape
    experts = lax.axis_size(("cp", "tp"))
    tp = lax.axis_size("tp")
    ep_size = lax.axis_size("ep")
    capacity = max(2, tokens * picks * 5 // (4 * experts))
    slots = experts * capacity
    width = output_cot.shape[1]
    blocks = width // LANES
    hidden = gate_weight.shape[2]
    tiled = slots * blocks
    place = lax.axis_index("ep").astype(jnp.int32).reshape(1)
    routes_t = routes.T
    gates_t = gate_values.T
    down_w = down_weight[0]
    gate_x = gate_weight.reshape(tp, ep_size, LANES, hidden)
    up_x = up_weight.reshape(tp, ep_size, LANES, hidden)
    gate_q = gate_weight.reshape(ep_size, width, hidden)
    up_q = up_weight.reshape(ep_size, width, hidden)
    shape = jax.ShapeDtypeStruct
    wide = pltpu.VMEM((tiled, LANES), F32)
    lhs = pltpu.VMEM((slots, width), BF)
    near = [(i, i ^ 1) for i in range(ep_size)]
    far = [(i, i ^ 2) for i in range(ep_size)]

    def exchange(rows):
        return lax.all_to_all(
            rows.reshape(experts, capacity * blocks, LANES),
            ("cp", "tp"),
            split_axis=0,
            concat_axis=0,
            tiled=True,
        ).reshape(tiled, LANES)

    moved = slots * width * 6
    dot_flops = 2 * slots * width * hidden
    acc = shape((slots, hidden), F32)
    send_t = shape((slots, width), BF)
    keep_t = shape((slots, width), F32)
    hid = shape((slots, hidden), BF)
    rows_t = shape((tiled, LANES), BF)

    quarter_x = lambda n: [
        pltpu.VMEM((n, tp, LANES, hidden), BF), pltpu.SemaphoreType.DMA((n,))
    ]
    quarter_q = lambda n: [pltpu.VMEM((n, width, hidden), BF), pltpu.SemaphoreType.DMA((n,))]
    quarter_d = lambda n: [pltpu.VMEM((n, hidden, width), BF), pltpu.SemaphoreType.DMA((n,))]

    x_cols = lax.all_to_all(
        layer_input.reshape(tp, tokens, LANES), "tp", split_axis=0, concat_axis=0, tiled=True
    )
    cot_rows = call(
        functools.partial(pack_cot_kernel, experts, capacity),
        [VMEM] * 3, shape((2, tiled, LANES), BF), [wide], 10**8, moved,
        routes_t, gates_t, output_cot,
    )
    x_rows = call(
        functools.partial(pack_input_kernel, experts, capacity),
        [VMEM] * 2 + [ANY], rows_t, [wide], 10**8, moved, routes_t, x_cols, cot_rows,
    )
    x0 = exchange(x_rows)
    x1 = lax.ppermute(x0, "ep", near)
    x2 = lax.ppermute(x0, "ep", far)
    chips = experts // tp
    groups = [
        [(z * tp + t) * ep_size + half * 2 + core
         for half in range(2) for z in range(chips) for t in range(tp)]
        for core in range(2)
    ]
    cot_here = lax.all_to_all(
        cot_rows.reshape(2 * experts, capacity * blocks, LANES),
        ("cp", "tp", "ep"), split_axis=0, concat_axis=0, tiled=True, axis_index_groups=groups,
    ).reshape(2, tiled, LANES)
    pre = call(
        pre_first_kernel, [SMEM] + [VMEM] * 2 + [HBM] * 2, [acc, acc],
        [wide, lhs, *quarter_x(4)], 4 * dot_flops, moved, place, x0, x1, gate_x, up_x,
    )
    x2 = tie(x2, *pre)
    x3 = lax.ppermute(x2, "ep", near)
    pre = call(
        pre_next_kernel, [SMEM] + [VMEM] * 3 + [HBM] * 2, [acc, acc],
        [wide, lhs, *quarter_x(2)], LONG, moved, place, x2, *pre, gate_x, up_x,
    )
    x_buf, x_sem = quarter_x(2)
    d_buf, d_sem = quarter_d(1)
    act, silu, dsilu, out_send = call(
        forward_kernel, [SMEM] + [VMEM] * 3 + [HBM] * 3, [hid, acc, acc, send_t],
        [wide, lhs, x_buf, d_buf, x_sem, d_sem],
        LONG, moved, place, x3, *pre, gate_x, up_x, down_w,
    )
    out_came = lax.ppermute(out_send, "ep", near)
    out_keep = call(
        keep_kernel, [SMEM, VMEM, HBM], keep_t, quarter_d(1), dot_flops, moved,
        place, act, down_w,
    )
    out_sum = call(
        chip_sum_kernel, [VMEM] * 2 + [ANY], send_t, [], 10**6, moved, out_keep, out_came, act
    )
    out_far = lax.ppermute(out_sum, "ep", far)
    out_send2, out_keep2 = call(
        own_out_kernel, [SMEM, VMEM, HBM], [send_t, keep_t], quarter_d(2),
        2 * dot_flops, moved, place, act, down_w,
    )
    cot_here = tie(cot_here, out_sum, out_keep2)
    cot_there = lax.ppermute(cot_here, "ep", near)
    d_part = call(
        dact_first_kernel, [SMEM, VMEM, HBM], acc, [wide, lhs, *quarter_d(2)],
        2 * dot_flops, moved, place, cot_here, down_w,
    )
    d_act = call(
        dact_last_kernel, [SMEM, VMEM, VMEM, HBM], acc, [wide, lhs, *quarter_d(2)],
        2 * dot_flops, moved, place, cot_there, d_part, down_w,
    )
    d_gate, d_up, grad_send, grad_keep = call(
        grad_kernel, [SMEM] + [VMEM] * 3 + [HBM] * 2, [hid, hid, send_t, keep_t], quarter_q(4),
        4 * dot_flops, moved, place, d_act, silu, dsilu, gate_q, up_q,
    )
    grad_came = lax.ppermute(grad_send, "ep", near)
    out_near = lax.ppermute(out_send2, "ep", near)
    grad_send2, grad_keep2 = call(
        own_grad_kernel, [SMEM] + [VMEM] * 2 + [HBM] * 2, [send_t, keep_t], quarter_q(4),
        4 * dot_flops, moved, place, d_gate, d_up, gate_q, up_q,
    )
    grad_near = lax.ppermute(grad_send2, "ep", near)
    grad_sum = call(
        chip_sum_kernel, [VMEM] * 2 + [ANY], send_t, [], 10**6, moved,
        grad_keep, grad_came, out_far,
    )
    grad_far = lax.ppermute(grad_sum, "ep", far)
    out_rows = call(
        finish_kernel, [VMEM] * 3 + [ANY], rows_t, [wide], 10**6, moved,
        out_keep2, out_near, out_far, grad_sum,
    )
    out_back = exchange(out_rows)
    grad_rows = call(
        finish_kernel, [VMEM] * 3 + [ANY], rows_t, [wide], LONG, moved,
        grad_keep2, grad_near, grad_far, out_rows,
    )
    grad_back = exchange(grad_rows)
    moe_output, gate_grad = call(
        functools.partial(combine_out_kernel, experts, capacity), [VMEM] * 4,
        [shape((tokens, width), BF), shape((tokens, picks), F32)], [wide, lhs], 10**8, moved,
        routes_t, gate_values, output_cot, out_back,
    )
    gate_grad = gate_grad + lax.ppermute(gate_grad, "ep", near)
    gate_grad = gate_grad + lax.ppermute(gate_grad, "ep", far)
    input_grad = call(
        functools.partial(combine_grad_kernel, experts, capacity), [VMEM] * 2,
        shape((tokens, width), BF), [wide, lhs], 10**8, moved,
        routes_t, grad_back,
    )
    return (moe_output, input_grad, gate_grad)


def solution(mesh):
    placed = (
        P("cp", ("tp", "ep")),
        P(("cp", "tp"), "ep"),
        P(("cp", "tp"), None),
        P(("cp", "tp"), None),
        P(("cp", "tp"), None, "ep"),
        P(("cp", "tp"), None, "ep"),
        P(("cp", "tp"), "ep", None),
    )
    return jax.shard_map(
        local,
        mesh=mesh,
        in_specs=placed,
        out_specs=(P(("cp", "tp"), "ep"), P(("cp", "tp"), "ep"), P(("cp", "tp"), None)),
        check_vma=False,
    )
```

```python
import functools

import jax
import jax.numpy as jnp
from jax import lax
from jax.experimental import pallas as pl
from jax.experimental.pallas import tpu as pltpu
from jax.sharding import PartitionSpec as P

BF = jnp.bfloat16
F32 = jnp.float32
LANES = 128
VMEM_BYTES = 20 * 1024 * 1024
RELAY = 4
SUMS = 2
LONG = 2 * 10**11


def nt(left, right):
    return lax.dot_general(
        left, right, (((1,), (1,)), ((), ())), preferred_element_type=F32
    )


def tn(left, right):
    return lax.dot_general(
        left, right, (((0,), (0,)), ((), ())), preferred_element_type=F32
    )


def slot_masks(routes, experts, capacity):
    picks, tokens = routes.shape
    expert = lax.broadcasted_iota(jnp.int32, (experts, tokens), 0)
    earlier = (
        lax.broadcasted_iota(jnp.int32, (tokens, tokens), 0)
        < lax.broadcasted_iota(jnp.int32, (tokens, tokens), 1)
    ).astype(F32).astype(BF)
    slot = lax.broadcasted_iota(jnp.int32, (experts * capacity, tokens), 0)
    taken = jnp.zeros((experts, 1), F32)
    masks = []
    for k in range(picks):
        named = routes[k : k + 1, :]
        chosen = (expert == named).astype(F32)
        before = jnp.dot(chosen.astype(BF), earlier, preferred_element_type=F32) + taken
        rank = jnp.sum(before * chosen, axis=0, keepdims=True)
        place = named * capacity + rank.astype(jnp.int32)
        masks.append((slot == place).astype(F32))
        taken = taken + jnp.sum(chosen, axis=1, keepdims=True)
    return masks


def tile_rows(values, blocks, wide_ref, out_ref):
    rows = wide_ref.shape[0] // blocks
    for f in range(blocks):
        wide_ref[pl.ds(f, rows, stride=blocks), :] = values(f)
    out_ref[...] = wide_ref[...].astype(BF)


def untile_rows(in_ref, blocks, wide_ref, out_ref):
    rows = wide_ref.shape[0] // blocks
    wide_ref[...] = in_ref[...].astype(F32)
    for f in range(blocks):
        out_ref[:, f * LANES : (f + 1) * LANES] = wide_ref[
            pl.ds(f, rows, stride=blocks), :
        ].astype(BF)


def pack_cot_kernel(
    experts, capacity, routes_ref, gates_ref, cot_ref, out_ref, token_ref, wide_ref
):
    masks = slot_masks(routes_ref[...], experts, capacity)
    both = functools.reduce(lambda a, b: a + b, masks)
    gate = functools.reduce(
        lambda a, b: a + b,
        [
            jnp.sum(m * gates_ref[k : k + 1, :], axis=1, keepdims=True)
            for k, m in enumerate(masks)
        ],
    )
    both = both.astype(BF)
    blocks = cot_ref.shape[1] // LANES

    def block(f):
        rows = jnp.dot(
            both, cot_ref[:, f * LANES : (f + 1) * LANES], preferred_element_type=F32
        )
        return rows * gate

    tile_rows(block, blocks, wide_ref, out_ref.at[0])
    out_ref[1] = out_ref[0]
    token_ref[...] = jnp.zeros_like(token_ref)


def pack_input_kernel(experts, capacity, routes_ref, x_ref, after, out_ref, wide_ref):
    masks = slot_masks(routes_ref[...], experts, capacity)
    both = functools.reduce(lambda a, b: a + b, masks).astype(BF)
    blocks = x_ref.shape[0]
    tile_rows(
        lambda f: jnp.dot(both, x_ref[f], preferred_element_type=F32),
        blocks,
        wide_ref,
        out_ref,
    )


def tie_kernel(x_ref, *rest):
    pass


def token_kernel(after, token_ref):
    token_ref[...] = jnp.zeros_like(token_ref)


def pieces_kernel(c, after, *outs):
    flat = c.shape[0] * c.shape[1] // len(outs)
    per = c.shape[1] // flat
    for i, out_ref in enumerate(outs):
        out_ref[...] = c[i // per, (i % per) * flat : (i % per + 1) * flat, :]


def untile_pieces(pieces, blocks, wide_ref, out_ref):
    at = 0
    for piece in pieces:
        wide_ref[at : at + piece.shape[0], :] = piece[...].astype(F32)
        at += piece.shape[0]
    rows = wide_ref.shape[0] // blocks
    for f in range(blocks):
        out_ref[:, f * LANES : (f + 1) * LANES] = wide_ref[
            pl.ds(f, rows, stride=blocks), :
        ].astype(BF)


def column_block(ref, index, width):
    return ref[:, pl.ds(pl.multiple_of(index * width, LANES), width)]


class Loads:
    def __init__(self, ref, indices, buffer, sems):
        width = buffer.shape[2]
        self.buffer = buffer
        self.copies = [
            pltpu.make_async_copy(
                ref.at[:, pl.ds(pl.multiple_of(index * width, LANES), width)],
                buffer.at[i],
                sems.at[i],
            )
            for i, index in enumerate(indices)
        ]
        for copy in self.copies:
            copy.start()

    def __getitem__(self, i):
        self.copies[i].wait()
        return self.buffer[i]


def dact_first_kernel(place_ref, *refs):
    *c, down, out_ref, wide, lhs, buffer, sems = refs
    core = place_ref[0] & 1
    w = Loads(down, (core, core + 2), buffer, sems)
    blocks = lhs.shape[1] // LANES
    half = len(c) // 2
    untile_pieces(c[:half], blocks, wide, lhs)
    out_ref[...] = nt(lhs[...], w[0])
    untile_pieces(c[half:], blocks, wide, lhs)
    out_ref[...] += nt(lhs[...], w[1])


def dact_last_kernel(place_ref, *refs):
    *c, part, down, out_ref, wide, lhs, buffer, sems = refs
    core = 1 - (place_ref[0] & 1)
    w = Loads(down, (core, core + 2), buffer, sems)
    blocks = lhs.shape[1] // LANES
    half = len(c) // 2
    untile_pieces(c[:half], blocks, wide, lhs)
    out_ref[...] = part[...] + nt(lhs[...], w[0])
    untile_pieces(c[half:], blocks, wide, lhs)
    out_ref[...] += nt(lhs[...], w[1])


def rows_block(ref, index, width):
    return ref[:, index].reshape(width, -1)


def pre_first_kernel(place_ref, x0, x1, gate, up, g_ref, u_ref, token_ref, wide, lhs):
    ep = place_ref[0]
    width = lhs.shape[1]
    untile_rows(x0, width // LANES, wide, lhs)
    g_ref[...] = jnp.dot(lhs[...], rows_block(gate, ep, width), preferred_element_type=F32)
    u_ref[...] = jnp.dot(lhs[...], rows_block(up, ep, width), preferred_element_type=F32)
    untile_rows(x1, width // LANES, wide, lhs)
    g_ref[...] += jnp.dot(lhs[...], rows_block(gate, ep ^ 1, width), preferred_element_type=F32)
    u_ref[...] += jnp.dot(lhs[...], rows_block(up, ep ^ 1, width), preferred_element_type=F32)
    token_ref[...] = jnp.zeros_like(token_ref)


def pre_next_kernel(place_ref, x2, g_in, u_in, gate, up, g_ref, u_ref, wide, lhs):
    ep = place_ref[0] ^ 2
    width = lhs.shape[1]
    untile_rows(x2, width // LANES, wide, lhs)
    g_ref[...] = g_in[...] + jnp.dot(
        lhs[...], rows_block(gate, ep, width), preferred_element_type=F32
    )
    u_ref[...] = u_in[...] + jnp.dot(
        lhs[...], rows_block(up, ep, width), preferred_element_type=F32
    )


def forward_kernel(
    place_ref, x3, g_in, u_in, gate, up, down,
    act_ref, silu_ref, dsilu_ref, send_ref, wide, lhs,
):
    ep = place_ref[0] ^ 3
    width = lhs.shape[1]
    untile_rows(x3, width // LANES, wide, lhs)
    pre_gate = g_in[...] + jnp.dot(
        lhs[...], rows_block(gate, ep, width), preferred_element_type=F32
    )
    pre_up = u_in[...] + jnp.dot(
        lhs[...], rows_block(up, ep, width), preferred_element_type=F32
    )
    sigmoid = jax.nn.sigmoid(pre_gate)
    silu = pre_gate * sigmoid
    silu_ref[...] = silu
    dsilu_ref[...] = pre_up * sigmoid * (1.0 + pre_gate * (1.0 - sigmoid))
    act_ref[...] = (silu * pre_up).astype(BF)
    send_ref[...] = jnp.dot(
        act_ref[...], column_block(down, ep, width), preferred_element_type=F32
    ).astype(BF)


def keep_kernel(place_ref, act_ref, down, keep_ref):
    keep_ref[...] = jnp.dot(
        act_ref[...],
        column_block(down, place_ref[0] ^ 2, keep_ref.shape[1]),
        preferred_element_type=F32,
    ).astype(BF)


def grad_block(dgate_ref, dup_ref, gate, up, index):
    return nt(dgate_ref[...], gate[index]) + nt(dup_ref[...], up[index])


def grad_kernel(
    place_ref, dact_ref, silu_ref, dsilu_ref, gate, up, dgate_ref, dup_ref, keep_ref, *sends
):
    ep = place_ref[0]
    d_act = dact_ref[...]
    dgate_ref[...] = (d_act * dsilu_ref[...]).astype(BF)
    dup_ref[...] = (d_act * silu_ref[...]).astype(BF)
    send = grad_block(dgate_ref, dup_ref, gate, up, ep ^ 3).astype(BF)
    for i, send_ref in enumerate(sends):
        part = send_ref.shape[1]
        send_ref[...] = send[:, i * part : (i + 1) * part]
    keep_ref[...] = grad_block(dgate_ref, dup_ref, gate, up, ep ^ 2).astype(BF)


def own_out_kernel(place_ref, act_ref, down, after, send_ref, keep_ref, token_ref):
    token_ref[...] = jnp.zeros_like(token_ref)
    ep = place_ref[0]
    width = send_ref.shape[1]
    send_ref[...] = jnp.dot(
        act_ref[...], column_block(down, ep ^ 1, width), preferred_element_type=F32
    ).astype(BF)
    keep_ref[...] = jnp.dot(
        act_ref[...], column_block(down, ep, width), preferred_element_type=F32
    ).astype(BF)


def own_grad_kernel(place_ref, dgate_ref, dup_ref, gate, up, after, send_ref, keep_ref):
    ep = place_ref[0]
    send_ref[...] = grad_block(dgate_ref, dup_ref, gate, up, ep ^ 1).astype(BF)
    keep_ref[...] = grad_block(dgate_ref, dup_ref, gate, up, ep).astype(BF)


def chip_sum_kernel(keep_ref, came_ref, after, out_ref, token_ref):
    token_ref[...] = jnp.zeros_like(token_ref)
    out_ref[...] = (keep_ref[...].astype(F32) + came_ref[...].astype(F32)).astype(BF)


def grad_sum_kernel(keep_ref, *refs):
    *came, after, out_ref, token_ref = refs
    token_ref[...] = jnp.zeros_like(token_ref)
    for i, ref in enumerate(came):
        cols = slice(i * ref.shape[1], (i + 1) * ref.shape[1])
        out_ref[:, cols] = (keep_ref[:, cols].astype(F32) + ref[...].astype(F32)).astype(BF)


def finish_kernel(keep_ref, near_ref, far_ref, after, out_ref, token_ref, wide_ref):
    token_ref[...] = jnp.zeros_like(token_ref)

    def block(f):
        cols = slice(f * LANES, (f + 1) * LANES)
        parts = [ref[:, cols].astype(F32) for ref in (keep_ref, near_ref, far_ref)]
        return parts[0] + parts[1] + parts[2]

    tile_rows(block, keep_ref.shape[1] // LANES, wide_ref, out_ref)


def combine_out_kernel(
    experts, capacity, routes_ref, gates_ref, cot_ref, rows_ref, out_ref, grad_ref, wide, lhs
):
    masks = slot_masks(routes_ref[...], experts, capacity)
    untile_rows(rows_ref, lhs.shape[1] // LANES, wide, lhs)
    cot = cot_ref[...].astype(F32)
    total = None
    grads = []
    for k, m in enumerate(masks):
        picked = tn(m.astype(BF), lhs[...])
        term = gates_ref[:, k : k + 1] * picked
        total = term if total is None else total + term
        grads.append(jnp.sum(cot * picked, axis=1, keepdims=True))
    out_ref[...] = total.astype(BF)
    grad_ref[...] = jnp.concatenate(grads, axis=1)


def combine_grad_kernel(experts, capacity, routes_ref, rows_ref, out_ref, wide, lhs):
    masks = slot_masks(routes_ref[...], experts, capacity)
    both = functools.reduce(lambda a, b: a + b, masks).astype(BF)
    untile_rows(rows_ref, lhs.shape[1] // LANES, wide, lhs)
    out_ref[...] = tn(both, lhs[...]).astype(BF)


SMEM = pl.BlockSpec(memory_space=pltpu.SMEM)
VMEM = pl.BlockSpec(memory_space=pltpu.VMEM)
ANY = pl.BlockSpec(memory_space=pl.ANY)
HBM = pl.BlockSpec(memory_space=pltpu.HBM)


def call(kernel, specs, outs, scratch, flops, moved, *operands):
    single = not isinstance(outs, (list, tuple))
    return pl.pallas_call(
        kernel,
        out_shape=outs,
        in_specs=specs,
        out_specs=VMEM if single else [VMEM] * len(outs),
        scratch_shapes=scratch,
        compiler_params=pltpu.CompilerParams(vmem_limit_bytes=VMEM_BYTES),
        cost_estimate=pl.CostEstimate(flops=flops, bytes_accessed=moved, transcendentals=0),
    )(*operands)


def tie(x, *after):
    return pl.pallas_call(
        tie_kernel,
        out_shape=jax.ShapeDtypeStruct(x.shape, x.dtype),
        in_specs=[ANY] * (1 + len(after)),
        out_specs=ANY,
        input_output_aliases={0: 0},
        compiler_params=pltpu.CompilerParams(vmem_limit_bytes=1024 * 1024),
    )(x, *after)


def local(layer_input, output_cot, routes, gate_values, gate_weight, up_weight, down_weight):
    tokens, picks = routes.shape
    experts = lax.axis_size(("cp", "tp"))
    tp = lax.axis_size("tp")
    ep_size = lax.axis_size("ep")
    capacity = max(2, tokens * picks * 5 // (4 * experts))
    slots = experts * capacity
    width = output_cot.shape[1]
    blocks = width // LANES
    hidden = gate_weight.shape[2]
    tiled = slots * blocks
    place = lax.axis_index("ep").astype(jnp.int32).reshape(1)
    routes_t = routes.T
    gates_t = gate_values.T
    down_w = down_weight[0]
    gate_x = gate_weight.reshape(tp, ep_size, LANES, hidden)
    up_x = up_weight.reshape(tp, ep_size, LANES, hidden)
    gate_q = gate_weight.reshape(ep_size, width, hidden)
    up_q = up_weight.reshape(ep_size, width, hidden)
    shape = jax.ShapeDtypeStruct
    wide = pltpu.VMEM((tiled, LANES), F32)
    lhs = pltpu.VMEM((slots, width), BF)
    near = [(i, i ^ 1) for i in range(ep_size)]
    far = [(i, i ^ 2) for i in range(ep_size)]

    def exchange(rows):
        return lax.all_to_all(
            rows.reshape(experts, capacity * blocks, LANES),
            ("cp", "tp"),
            split_axis=0,
            concat_axis=0,
            tiled=True,
        ).reshape(tiled, LANES)

    moved = slots * width * 6
    dot_flops = 2 * slots * width * hidden
    acc = shape((slots, hidden), F32)
    send_t = shape((slots, width), BF)
    keep_t = shape((slots, width), BF)
    hid = shape((slots, hidden), BF)
    rows_t = shape((tiled, LANES), BF)

    token = shape((8, LANES), F32)
    loads = [pltpu.VMEM((2, hidden, width), BF), pltpu.SemaphoreType.DMA((2,))]

    x_cols = lax.all_to_all(
        layer_input.reshape(tp, tokens, LANES), "tp", split_axis=0, concat_axis=0, tiled=True
    )
    cot_rows, cot_token = call(
        functools.partial(pack_cot_kernel, experts, capacity),
        [VMEM] * 3, [shape((2, tiled, LANES), BF), token], [wide], 10**8, moved,
        routes_t, gates_t, output_cot,
    )
    x_rows = call(
        functools.partial(pack_input_kernel, experts, capacity),
        [VMEM] * 3, rows_t, [wide], 10**8, moved, routes_t, x_cols, cot_token,
    )
    x0 = exchange(x_rows)
    x1 = lax.ppermute(x0, "ep", near)
    x2 = lax.ppermute(x0, "ep", far)
    chips = experts // tp
    groups = [
        [(z * tp + t) * ep_size + half * 2 + core
         for half in range(2) for z in range(chips) for t in range(tp)]
        for core in range(2)
    ]
    cot_here = lax.all_to_all(
        cot_rows.reshape(2 * experts, capacity * blocks, LANES),
        ("cp", "tp", "ep"), split_axis=0, concat_axis=0, tiled=True, axis_index_groups=groups,
    ).reshape(2, tiled, LANES)
    *pre, p_token = call(
        pre_first_kernel, [SMEM] + [VMEM] * 4, [acc, acc, token],
        [wide, lhs], 4 * dot_flops, moved, place, x0, x1, gate_x, up_x,
    )
    x2 = tie(x2, p_token)
    x3 = lax.ppermute(x2, "ep", near)
    pre = call(
        pre_next_kernel, [SMEM] + [VMEM] * 3 + [VMEM] * 2, [acc, acc],
        [wide, lhs], LONG, moved, place, x2, *pre, gate_x, up_x,
    )
    act, silu, dsilu, out_send = call(
        forward_kernel, [SMEM] + [VMEM] * 3 + [VMEM] * 3, [hid, acc, acc, send_t],
        [wide, lhs],
        LONG, moved, place, x3, *pre, gate_x, up_x, down_w,
    )
    out_came = lax.ppermute(out_send, "ep", near)
    out_keep = call(
        keep_kernel, [SMEM, VMEM, VMEM], keep_t, [], dot_flops, moved,
        place, act, down_w,
    )
    out_sum, out_token = call(
        chip_sum_kernel, [VMEM] * 2 + [ANY], [send_t, token], [], 10**6, moved,
        out_keep, out_came, p_token,
    )
    out_far = lax.ppermute(out_sum, "ep", far)
    out_send2, out_keep2, own_token = call(
        own_out_kernel, [SMEM, VMEM, VMEM, ANY], [send_t, keep_t, token], [],
        2 * dot_flops, moved, place, act, down_w, out_token,
    )
    cot_here = call(
        pieces_kernel, [VMEM, ANY], [shape((2 * tiled // RELAY, LANES), BF)] * RELAY, [],
        10**6, moved, cot_here, own_token,
    )
    cot_there = [lax.ppermute(piece, "ep", near) for piece in cot_here]
    d_part = call(
        dact_first_kernel, [SMEM] + [VMEM] * RELAY + [HBM], acc, [wide, lhs, *loads],
        2 * dot_flops, moved, place, *cot_here, down_w,
    )
    far_token = call(token_kernel, [ANY], token, [], LONG, 10**4, out_far)
    d_act = call(
        dact_last_kernel, [SMEM] + [VMEM] * (RELAY + 1) + [HBM], acc, [wide, lhs, *loads],
        2 * dot_flops, moved, place, *cot_there, d_part, down_w,
    )
    d_gate, d_up, grad_keep, *grad_sends = call(
        grad_kernel, [SMEM] + [VMEM] * 3 + [VMEM] * 2, [hid, hid, keep_t] + [shape((slots, width // SUMS), BF)] * SUMS, [],
        4 * dot_flops, moved, place, d_act, silu, dsilu, gate_q, up_q,
    )
    grad_came = [lax.ppermute(send, "ep", near) for send in grad_sends]
    out_near = lax.ppermute(out_send2, "ep", near)
    out_rows, rows_token = call(
        finish_kernel, [VMEM] * 3 + [ANY], [rows_t, token], [wide], 10**6, moved,
        out_keep2, out_near, out_far, far_token,
    )
    grad_sum, g_token = call(
        grad_sum_kernel, [VMEM] * (SUMS + 1) + [ANY], [send_t, token], [], 10**6, moved,
        grad_keep, *grad_came, rows_token,
    )
    grad_far = lax.ppermute(grad_sum, "ep", far)
    grad_send2, grad_keep2 = call(
        own_grad_kernel, [SMEM] + [VMEM] * 4 + [ANY], [send_t, keep_t], [],
        4 * dot_flops, moved, place, d_gate, d_up, gate_q, up_q, g_token,
    )
    grad_near = lax.ppermute(grad_send2, "ep", near)
    out_back = exchange(out_rows)
    last_token = call(token_kernel, [ANY], token, [], LONG, 10**4, grad_far)
    grad_rows, _ = call(
        finish_kernel, [VMEM] * 3 + [ANY], [rows_t, token], [wide], 10**6, moved,
        grad_keep2, grad_near, grad_far, last_token,
    )
    grad_back = exchange(grad_rows)
    moe_output, gate_grad = call(
        functools.partial(combine_out_kernel, experts, capacity), [VMEM] * 4,
        [shape((tokens, width), BF), shape((tokens, picks), F32)], [wide, lhs], 10**8, moved,
        routes_t, gate_values, output_cot, out_back,
    )
    gate_grad = gate_grad + lax.ppermute(gate_grad, "ep", near)
    gate_grad = gate_grad + lax.ppermute(gate_grad, "ep", far)
    input_grad = call(
        functools.partial(combine_grad_kernel, experts, capacity), [VMEM] * 2,
        shape((tokens, width), BF), [wide, lhs], 10**8, moved,
        routes_t, grad_back,
    )
    return (moe_output, input_grad, gate_grad)


def solution(mesh):
    placed = (
        P("cp", ("tp", "ep")),
        P(("cp", "tp"), "ep"),
        P(("cp", "tp"), None),
        P(("cp", "tp"), None),
        P(("cp", "tp"), None, "ep"),
        P(("cp", "tp"), None, "ep"),
        P(("cp", "tp"), "ep", None),
    )
    return jax.shard_map(
        local,
        mesh=mesh,
        in_specs=placed,
        out_specs=(P(("cp", "tp"), "ep"), P(("cp", "tp"), "ep"), P(("cp", "tp"), None)),
        check_vma=False,
    )
```

```python
import functools

import jax
import jax.numpy as jnp
from jax import lax
from jax.experimental import pallas as pl
from jax.experimental.pallas import tpu as pltpu
from jax.sharding import PartitionSpec as P

BF = jnp.bfloat16
F32 = jnp.float32
LANES = 128
VMEM_BYTES = 20 * 1024 * 1024
RELAY = 4
SUMS = 2
LONG = 2 * 10**11


def nt(left, right):
    return lax.dot_general(
        left, right, (((1,), (1,)), ((), ())), preferred_element_type=F32
    )


def tn(left, right):
    return lax.dot_general(
        left, right, (((0,), (0,)), ((), ())), preferred_element_type=F32
    )


def slot_masks(routes, experts, capacity):
    picks, tokens = routes.shape
    expert = lax.broadcasted_iota(jnp.int32, (experts, tokens), 0)
    earlier = (
        lax.broadcasted_iota(jnp.int32, (tokens, tokens), 0)
        < lax.broadcasted_iota(jnp.int32, (tokens, tokens), 1)
    ).astype(F32).astype(BF)
    slot = lax.broadcasted_iota(jnp.int32, (experts * capacity, tokens), 0)
    taken = jnp.zeros((experts, 1), F32)
    masks = []
    for k in range(picks):
        named = routes[k : k + 1, :]
        chosen = (expert == named).astype(F32)
        before = jnp.dot(chosen.astype(BF), earlier, preferred_element_type=F32) + taken
        rank = jnp.sum(before * chosen, axis=0, keepdims=True)
        place = named * capacity + rank.astype(jnp.int32)
        masks.append((slot == place).astype(F32))
        taken = taken + jnp.sum(chosen, axis=1, keepdims=True)
    return masks


def tile_rows(values, blocks, wide_ref, out_ref):
    rows = wide_ref.shape[0] // blocks
    for f in range(blocks):
        wide_ref[pl.ds(f, rows, stride=blocks), :] = values(f)
    out_ref[...] = wide_ref[...].astype(BF)


def untile_rows(in_ref, blocks, wide_ref, out_ref):
    rows = wide_ref.shape[0] // blocks
    wide_ref[...] = in_ref[...].astype(F32)
    for f in range(blocks):
        out_ref[:, f * LANES : (f + 1) * LANES] = wide_ref[
            pl.ds(f, rows, stride=blocks), :
        ].astype(BF)


def pack_cot_kernel(
    experts, capacity, routes_ref, gates_ref, cot_ref, out_ref, token_ref, wide_ref
):
    masks = slot_masks(routes_ref[...], experts, capacity)
    both = functools.reduce(lambda a, b: a + b, masks)
    gate = functools.reduce(
        lambda a, b: a + b,
        [
            jnp.sum(m * gates_ref[k : k + 1, :], axis=1, keepdims=True)
            for k, m in enumerate(masks)
        ],
    )
    both = both.astype(BF)
    blocks = cot_ref.shape[1] // LANES

    def block(f):
        rows = jnp.dot(
            both, cot_ref[:, f * LANES : (f + 1) * LANES], preferred_element_type=F32
        )
        return rows * gate

    tile_rows(block, blocks, wide_ref, out_ref.at[0])
    out_ref[1] = out_ref[0]
    token_ref[...] = jnp.zeros_like(token_ref)


def pack_input_kernel(experts, capacity, routes_ref, x_ref, after, out_ref, wide_ref):
    masks = slot_masks(routes_ref[...], experts, capacity)
    both = functools.reduce(lambda a, b: a + b, masks).astype(BF)
    blocks = x_ref.shape[0]
    tile_rows(
        lambda f: jnp.dot(both, x_ref[f], preferred_element_type=F32),
        blocks,
        wide_ref,
        out_ref,
    )


def tie_kernel(x_ref, *rest):
    pass


def token_kernel(after, token_ref):
    token_ref[...] = jnp.zeros_like(token_ref)


def split_kernel(x_ref, *outs):
    rows = outs[0].shape[0]
    for i, out_ref in enumerate(outs):
        out_ref[...] = x_ref[i * rows : (i + 1) * rows, :]


def pieces_kernel(c, after, *refs):
    *outs, sems = refs
    flat = c.shape[0] * c.shape[1] // len(outs)
    per = c.shape[1] // flat
    copies = [
        pltpu.make_async_copy(
            c.at[i // per, pl.ds((i % per) * flat, flat)], out_ref, sems.at[i]
        )
        for i, out_ref in enumerate(outs)
    ]
    for copy in copies:
        copy.start()
    for copy in copies:
        copy.wait()


def untile_pieces(pieces, blocks, wide_ref, out_ref):
    at = 0
    for piece in pieces:
        wide_ref[at : at + piece.shape[0], :] = piece[...].astype(F32)
        at += piece.shape[0]
    rows = wide_ref.shape[0] // blocks
    for f in range(blocks):
        out_ref[:, f * LANES : (f + 1) * LANES] = wide_ref[
            pl.ds(f, rows, stride=blocks), :
        ].astype(BF)


def column_block(ref, index, width):
    return ref[:, pl.ds(pl.multiple_of(index * width, LANES), width)]


class Loads:
    def __init__(self, ref, indices, buffer, sems):
        width = buffer.shape[2]
        self.buffer = buffer
        self.copies = [
            pltpu.make_async_copy(
                ref.at[:, pl.ds(pl.multiple_of(index * width, LANES), width)],
                buffer.at[i],
                sems.at[i],
            )
            for i, index in enumerate(indices)
        ]
        for copy in self.copies:
            copy.start()

    def __getitem__(self, i):
        self.copies[i].wait()
        return self.buffer[i]


def dact_first_kernel(place_ref, *refs):
    *c, down, out_ref, wide, lhs = refs
    core = place_ref[0] & 1
    w = [column_block(down, core + 2 * j, lhs.shape[1]) for j in range(2)]
    blocks = lhs.shape[1] // LANES
    half = len(c) // 2
    untile_pieces(c[:half], blocks, wide, lhs)
    out_ref[...] = nt(lhs[...], w[0])
    untile_pieces(c[half:], blocks, wide, lhs)
    out_ref[...] += nt(lhs[...], w[1])


def dact_last_kernel(place_ref, *refs):
    *c, part, down, out_ref, wide, lhs = refs
    core = 1 - (place_ref[0] & 1)
    w = [column_block(down, core + 2 * j, lhs.shape[1]) for j in range(2)]
    blocks = lhs.shape[1] // LANES
    half = len(c) // 2
    untile_pieces(c[:half], blocks, wide, lhs)
    out_ref[...] = part[...] + nt(lhs[...], w[0])
    untile_pieces(c[half:], blocks, wide, lhs)
    out_ref[...] += nt(lhs[...], w[1])


def rows_block(ref, index, width):
    return ref[:, index].reshape(width, -1)


def pre_first_kernel(place_ref, x0, gate, up, g_ref, u_ref, wide, lhs):
    ep = place_ref[0]
    width = lhs.shape[1]
    untile_rows(x0, width // LANES, wide, lhs)
    g_ref[...] = jnp.dot(lhs[...], rows_block(gate, ep, width), preferred_element_type=F32)
    u_ref[...] = jnp.dot(lhs[...], rows_block(up, ep, width), preferred_element_type=F32)


def pre_beside_kernel(place_ref, *refs):
    *x1, g_in, u_in, gate, up, g_ref, u_ref, token_ref, wide, lhs = refs
    ep = place_ref[0] ^ 1
    width = lhs.shape[1]
    untile_pieces(x1, width // LANES, wide, lhs)
    g_ref[...] = g_in[...] + jnp.dot(
        lhs[...], rows_block(gate, ep, width), preferred_element_type=F32
    )
    u_ref[...] = u_in[...] + jnp.dot(
        lhs[...], rows_block(up, ep, width), preferred_element_type=F32
    )
    token_ref[...] = jnp.zeros_like(token_ref)


def pre_next_kernel(place_ref, x2, g_in, u_in, gate, up, g_ref, u_ref, wide, lhs):
    ep = place_ref[0] ^ 2
    width = lhs.shape[1]
    untile_rows(x2, width // LANES, wide, lhs)
    g_ref[...] = g_in[...] + jnp.dot(
        lhs[...], rows_block(gate, ep, width), preferred_element_type=F32
    )
    u_ref[...] = u_in[...] + jnp.dot(
        lhs[...], rows_block(up, ep, width), preferred_element_type=F32
    )


def forward_kernel(
    place_ref, x3, g_in, u_in, gate, up, down,
    act_ref, silu_ref, dsilu_ref, send_ref, wide, lhs,
):
    ep = place_ref[0] ^ 3
    width = lhs.shape[1]
    untile_rows(x3, width // LANES, wide, lhs)
    pre_gate = g_in[...] + jnp.dot(
        lhs[...], rows_block(gate, ep, width), preferred_element_type=F32
    )
    pre_up = u_in[...] + jnp.dot(
        lhs[...], rows_block(up, ep, width), preferred_element_type=F32
    )
    sigmoid = jax.nn.sigmoid(pre_gate)
    silu = pre_gate * sigmoid
    silu_ref[...] = silu
    dsilu_ref[...] = pre_up * sigmoid * (1.0 + pre_gate * (1.0 - sigmoid))
    act_ref[...] = (silu * pre_up).astype(BF)
    send_ref[...] = jnp.dot(
        act_ref[...], column_block(down, ep, width), preferred_element_type=F32
    ).astype(BF)


def keep_kernel(place_ref, act_ref, down, keep_ref):
    keep_ref[...] = jnp.dot(
        act_ref[...],
        column_block(down, place_ref[0] ^ 2, keep_ref.shape[1]),
        preferred_element_type=F32,
    ).astype(BF)


def grad_block(dgate_ref, dup_ref, gate, up, index):
    return nt(dgate_ref[...], gate[index]) + nt(dup_ref[...], up[index])


def grad_kernel(
    place_ref, dact_ref, silu_ref, dsilu_ref, gate, up, dgate_ref, dup_ref, keep_ref, *sends
):
    ep = place_ref[0]
    d_act = dact_ref[...]
    dgate_ref[...] = (d_act * dsilu_ref[...]).astype(BF)
    dup_ref[...] = (d_act * silu_ref[...]).astype(BF)
    send = grad_block(dgate_ref, dup_ref, gate, up, ep ^ 3).astype(BF)
    for i, send_ref in enumerate(sends):
        part = send_ref.shape[1]
        send_ref[...] = send[:, i * part : (i + 1) * part]
    keep_ref[...] = grad_block(dgate_ref, dup_ref, gate, up, ep ^ 2).astype(BF)


def own_out_kernel(place_ref, act_ref, down, after, send_ref, keep_ref, token_ref):
    token_ref[...] = jnp.zeros_like(token_ref)
    ep = place_ref[0]
    width = send_ref.shape[1]
    send_ref[...] = jnp.dot(
        act_ref[...], column_block(down, ep ^ 1, width), preferred_element_type=F32
    ).astype(BF)
    keep_ref[...] = jnp.dot(
        act_ref[...], column_block(down, ep, width), preferred_element_type=F32
    ).astype(BF)


def own_grad_kernel(place_ref, dgate_ref, dup_ref, gate, up, after, send_ref, keep_ref):
    ep = place_ref[0]
    send_ref[...] = grad_block(dgate_ref, dup_ref, gate, up, ep ^ 1).astype(BF)
    keep_ref[...] = grad_block(dgate_ref, dup_ref, gate, up, ep).astype(BF)


def chip_sum_kernel(keep_ref, came_ref, after, out_ref, token_ref):
    token_ref[...] = jnp.zeros_like(token_ref)
    out_ref[...] = (keep_ref[...].astype(F32) + came_ref[...].astype(F32)).astype(BF)


def finish_out_kernel(keep_ref, near_ref, far_ref, grad_ref, *refs):
    *came, after, out_ref, sum_ref, token_ref, wide_ref, sum_buf, rows_buf, sems = refs
    token_ref[...] = jnp.zeros_like(token_ref)
    for i, ref in enumerate(came):
        cols = slice(i * ref.shape[1], (i + 1) * ref.shape[1])
        sum_buf[:, cols] = (grad_ref[:, cols].astype(F32) + ref[...].astype(F32)).astype(BF)
    sum_copy = pltpu.make_async_copy(sum_buf, sum_ref, sems.at[0])
    sum_copy.start()

    def block(f):
        cols = slice(f * LANES, (f + 1) * LANES)
        parts = [ref[:, cols].astype(F32) for ref in (keep_ref, near_ref, far_ref)]
        return parts[0] + parts[1] + parts[2]

    tile_rows(block, keep_ref.shape[1] // LANES, wide_ref, rows_buf)
    rows_copy = pltpu.make_async_copy(rows_buf, out_ref, sems.at[1])
    rows_copy.start()
    sum_copy.wait()
    rows_copy.wait()


def finish_kernel(keep_ref, near_ref, far_ref, after, out_ref, token_ref, wide_ref):
    token_ref[...] = jnp.zeros_like(token_ref)

    def block(f):
        cols = slice(f * LANES, (f + 1) * LANES)
        parts = [ref[:, cols].astype(F32) for ref in (keep_ref, near_ref, far_ref)]
        return parts[0] + parts[1] + parts[2]

    tile_rows(block, keep_ref.shape[1] // LANES, wide_ref, out_ref)


def combine_out_kernel(
    experts, capacity, routes_ref, gates_ref, cot_ref, rows_ref, out_ref, grad_ref, wide, lhs
):
    masks = slot_masks(routes_ref[...], experts, capacity)
    untile_rows(rows_ref, lhs.shape[1] // LANES, wide, lhs)
    cot = cot_ref[...].astype(F32)
    total = None
    grads = []
    for k, m in enumerate(masks):
        picked = tn(m.astype(BF), lhs[...])
        term = gates_ref[:, k : k + 1] * picked
        total = term if total is None else total + term
        grads.append(jnp.sum(cot * picked, axis=1, keepdims=True))
    out_ref[...] = total.astype(BF)
    grad_ref[...] = jnp.concatenate(grads, axis=1)


def combine_grad_kernel(experts, capacity, routes_ref, rows_ref, out_ref, wide, lhs):
    masks = slot_masks(routes_ref[...], experts, capacity)
    both = functools.reduce(lambda a, b: a + b, masks).astype(BF)
    untile_rows(rows_ref, lhs.shape[1] // LANES, wide, lhs)
    out_ref[...] = tn(both, lhs[...]).astype(BF)


SMEM = pl.BlockSpec(memory_space=pltpu.SMEM)
VMEM = pl.BlockSpec(memory_space=pltpu.VMEM)
ANY = pl.BlockSpec(memory_space=pl.ANY)
HBM = pl.BlockSpec(memory_space=pltpu.HBM)


def call(kernel, specs, outs, scratch, flops, moved, *operands, place_outs=None):
    single = not isinstance(outs, (list, tuple))
    return pl.pallas_call(
        kernel,
        out_shape=outs,
        in_specs=specs,
        out_specs=place_outs or (VMEM if single else [VMEM] * len(outs)),
        scratch_shapes=scratch,
        compiler_params=pltpu.CompilerParams(vmem_limit_bytes=VMEM_BYTES),
        cost_estimate=pl.CostEstimate(flops=flops, bytes_accessed=moved, transcendentals=0),
    )(*operands)


def tie(x, *after):
    return pl.pallas_call(
        tie_kernel,
        out_shape=jax.ShapeDtypeStruct(x.shape, x.dtype),
        in_specs=[ANY] * (1 + len(after)),
        out_specs=ANY,
        input_output_aliases={0: 0},
        compiler_params=pltpu.CompilerParams(vmem_limit_bytes=1024 * 1024),
    )(x, *after)


def local(layer_input, output_cot, routes, gate_values, gate_weight, up_weight, down_weight):
    tokens, picks = routes.shape
    experts = lax.axis_size(("cp", "tp"))
    tp = lax.axis_size("tp")
    ep_size = lax.axis_size("ep")
    capacity = max(2, tokens * picks * 5 // (4 * experts))
    slots = experts * capacity
    width = output_cot.shape[1]
    blocks = width // LANES
    hidden = gate_weight.shape[2]
    tiled = slots * blocks
    place = lax.axis_index("ep").astype(jnp.int32).reshape(1)
    routes_t = routes.T
    gates_t = gate_values.T
    down_w = down_weight[0]
    gate_x = gate_weight.reshape(tp, ep_size, LANES, hidden)
    up_x = up_weight.reshape(tp, ep_size, LANES, hidden)
    gate_q = gate_weight.reshape(ep_size, width, hidden)
    up_q = up_weight.reshape(ep_size, width, hidden)
    shape = jax.ShapeDtypeStruct
    wide = pltpu.VMEM((tiled, LANES), F32)
    lhs = pltpu.VMEM((slots, width), BF)
    near = [(i, i ^ 1) for i in range(ep_size)]
    far = [(i, i ^ 2) for i in range(ep_size)]

    def exchange(rows):
        return lax.all_to_all(
            rows.reshape(experts, capacity * blocks, LANES),
            ("cp", "tp"),
            split_axis=0,
            concat_axis=0,
            tiled=True,
        ).reshape(tiled, LANES)

    moved = slots * width * 6
    dot_flops = 2 * slots * width * hidden
    acc = shape((slots, hidden), F32)
    send_t = shape((slots, width), BF)
    keep_t = shape((slots, width), BF)
    hid = shape((slots, hidden), BF)
    rows_t = shape((tiled, LANES), BF)

    token = shape((8, LANES), F32)
    loads = [pltpu.VMEM((2, hidden, width), BF), pltpu.SemaphoreType.DMA((2,))]

    x_cols = lax.all_to_all(
        layer_input.reshape(tp, tokens, LANES), "tp", split_axis=0, concat_axis=0, tiled=True
    )
    cot_rows, cot_token = call(
        functools.partial(pack_cot_kernel, experts, capacity),
        [VMEM] * 3, [shape((2, tiled, LANES), BF), token], [wide], 10**8, moved,
        routes_t, gates_t, output_cot,
    )
    x_rows = call(
        functools.partial(pack_input_kernel, experts, capacity),
        [VMEM] * 3, rows_t, [wide], 10**8, moved, routes_t, x_cols, cot_token,
    )
    x0 = exchange(x_rows)
    x2 = lax.ppermute(x0, "ep", far)
    chips = experts // tp
    groups = [
        [(z * tp + t) * ep_size + half * 2 + core
         for half in range(2) for z in range(chips) for t in range(tp)]
        for core in range(2)
    ]
    cot_here = lax.all_to_all(
        cot_rows.reshape(2 * experts, capacity * blocks, LANES),
        ("cp", "tp", "ep"), split_axis=0, concat_axis=0, tiled=True, axis_index_groups=groups,
    ).reshape(2, tiled, LANES)
    pre = call(
        pre_first_kernel, [SMEM] + [VMEM] * 3, [acc, acc], [wide, lhs],
        2 * dot_flops, moved, place, x0, gate_x, up_x,
    )
    x1 = call(
        split_kernel, [VMEM], [shape((tiled // RELAY, LANES), BF)] * RELAY, [], 10**6, moved, x0
    )
    x1 = [lax.ppermute(piece, "ep", near) for piece in x1]
    *pre, p_token = call(
        pre_beside_kernel, [SMEM] + [VMEM] * (RELAY + 4), [acc, acc, token], [wide, lhs],
        2 * dot_flops, moved, place, *x1, *pre, gate_x, up_x,
    )
    x2 = tie(x2, p_token)
    x3 = lax.ppermute(x2, "ep", near)
    pre = call(
        pre_next_kernel, [SMEM] + [VMEM] * 3 + [VMEM] * 2, [acc, acc],
        [wide, lhs], 12000000000, moved, place, x2, *pre, gate_x, up_x,
    )
    act, silu, dsilu, out_send = call(
        forward_kernel, [SMEM] + [VMEM] * 3 + [VMEM] * 3, [hid, acc, acc, send_t],
        [wide, lhs],
        3 * dot_flops, moved, place, x3, *pre, gate_x, up_x, down_w,
    )
    out_came = lax.ppermute(out_send, "ep", near)
    out_keep = call(
        keep_kernel, [SMEM, VMEM, VMEM], keep_t, [], dot_flops, moved,
        place, act, down_w,
    )
    out_sum, out_token = call(
        chip_sum_kernel, [VMEM] * 2 + [ANY], [send_t, token], [], 10**6, moved,
        out_keep, out_came, p_token,
    )
    out_far = lax.ppermute(out_sum, "ep", far)
    out_send2, out_keep2, own_token = call(
        own_out_kernel, [SMEM, VMEM, VMEM, ANY], [send_t, keep_t, token], [],
        2 * dot_flops, moved, place, act, down_w, out_token,
    )
    cot_here = call(
        pieces_kernel, [ANY, ANY], [shape((2 * tiled // RELAY, LANES), BF)] * RELAY,
        [pltpu.SemaphoreType.DMA((RELAY,))], 10**6, moved, cot_here, own_token,
        place_outs=[ANY] * RELAY,
    )
    cot_there = [lax.ppermute(piece, "ep", near) for piece in cot_here]
    d_part = call(
        dact_first_kernel, [SMEM] + [VMEM] * (RELAY + 1), acc, [wide, lhs],
        2 * dot_flops, moved, place, *cot_here, down_w,
    )
    far_token = call(token_kernel, [ANY], token, [], LONG, 10**4, out_far)
    d_act = call(
        dact_last_kernel, [SMEM] + [VMEM] * (RELAY + 2), acc, [wide, lhs],
        2 * dot_flops, moved, place, *cot_there, d_part, down_w,
    )
    d_gate, d_up, grad_keep, *grad_sends = call(
        grad_kernel, [SMEM] + [VMEM] * 3 + [VMEM] * 2, [hid, hid, keep_t] + [shape((slots, width // SUMS), BF)] * SUMS, [],
        4 * dot_flops, moved, place, d_act, silu, dsilu, gate_q, up_q,
    )
    grad_came = [lax.ppermute(send, "ep", near) for send in grad_sends]
    out_near = lax.ppermute(out_send2, "ep", near)
    out_rows, grad_sum, g_token = call(
        finish_out_kernel, [VMEM] * (SUMS + 4) + [ANY], [rows_t, send_t, token],
        [wide, pltpu.VMEM((slots, width), BF), pltpu.VMEM((tiled, LANES), BF),
         pltpu.SemaphoreType.DMA((2,))],
        10**6, 2 * moved, out_keep2, out_near, out_far, grad_keep, *grad_came, far_token,
        place_outs=[ANY, ANY, VMEM],
    )
    grad_far = lax.ppermute(grad_sum, "ep", far)
    grad_send2, grad_keep2 = call(
        own_grad_kernel, [SMEM] + [VMEM] * 4 + [ANY], [send_t, keep_t], [],
        4 * dot_flops, moved, place, d_gate, d_up, gate_q, up_q, g_token,
    )
    grad_near = lax.ppermute(grad_send2, "ep", near)
    out_back = exchange(out_rows)
    last_token = call(token_kernel, [ANY], token, [], LONG, 10**4, grad_far)
    grad_rows, _ = call(
        finish_kernel, [VMEM] * 3 + [ANY], [rows_t, token], [wide], 10**6, moved,
        grad_keep2, grad_near, grad_far, last_token,
    )
    grad_back = exchange(grad_rows)
    moe_output, gate_grad = call(
        functools.partial(combine_out_kernel, experts, capacity), [VMEM] * 4,
        [shape((tokens, width), BF), shape((tokens, picks), F32)], [wide, lhs], 10**8, moved,
        routes_t, gate_values, output_cot, out_back,
    )
    gate_grad = gate_grad + lax.ppermute(gate_grad, "ep", near)
    gate_grad = gate_grad + lax.ppermute(gate_grad, "ep", far)
    input_grad = call(
        functools.partial(combine_grad_kernel, experts, capacity), [VMEM] * 2,
        shape((tokens, width), BF), [wide, lhs], 10**8, moved,
        routes_t, grad_back,
    )
    return (moe_output, input_grad, gate_grad)


def solution(mesh):
    placed = (
        P("cp", ("tp", "ep")),
        P(("cp", "tp"), "ep"),
        P(("cp", "tp"), None),
        P(("cp", "tp"), None),
        P(("cp", "tp"), None, "ep"),
        P(("cp", "tp"), None, "ep"),
        P(("cp", "tp"), "ep", None),
    )
    return jax.shard_map(
        local,
        mesh=mesh,
        in_specs=placed,
        out_specs=(P(("cp", "tp"), "ep"), P(("cp", "tp"), "ep"), P(("cp", "tp"), None)),
        check_vma=False,
    )
```

```python
import functools

import jax
import jax.numpy as jnp
from jax import lax
from jax.experimental import pallas as pl
from jax.experimental.pallas import tpu as pltpu
from jax.sharding import PartitionSpec as P

BF = jnp.bfloat16
F32 = jnp.float32
LANES = 128
VMEM_BYTES = 20 * 1024 * 1024
RELAY = 4
SUMS = 2
LONG = 2 * 10**11


def nt(left, right):
    return lax.dot_general(
        left, right, (((1,), (1,)), ((), ())), preferred_element_type=F32
    )


def tn(left, right):
    return lax.dot_general(
        left, right, (((0,), (0,)), ((), ())), preferred_element_type=F32
    )


def slot_masks(routes, experts, capacity):
    picks, tokens = routes.shape
    expert = lax.broadcasted_iota(jnp.int32, (experts, tokens), 0)
    earlier = (
        lax.broadcasted_iota(jnp.int32, (tokens, tokens), 0)
        < lax.broadcasted_iota(jnp.int32, (tokens, tokens), 1)
    ).astype(F32).astype(BF)
    slot = lax.broadcasted_iota(jnp.int32, (experts * capacity, tokens), 0)
    taken = jnp.zeros((experts, 1), F32)
    masks = []
    for k in range(picks):
        named = routes[k : k + 1, :]
        chosen = (expert == named).astype(F32)
        before = jnp.dot(chosen.astype(BF), earlier, preferred_element_type=F32) + taken
        rank = jnp.sum(before * chosen, axis=0, keepdims=True)
        place = named * capacity + rank.astype(jnp.int32)
        masks.append((slot == place).astype(F32))
        taken = taken + jnp.sum(chosen, axis=1, keepdims=True)
    return masks


def tile_rows(values, blocks, wide_ref, out_ref):
    rows = wide_ref.shape[0] // blocks
    for f in range(blocks):
        wide_ref[pl.ds(f, rows, stride=blocks), :] = values(f)
    out_ref[...] = wide_ref[...].astype(BF)


def untile_rows(in_ref, blocks, wide_ref, out_ref):
    rows = wide_ref.shape[0] // blocks
    wide_ref[...] = in_ref[...].astype(F32)
    for f in range(blocks):
        out_ref[:, f * LANES : (f + 1) * LANES] = wide_ref[
            pl.ds(f, rows, stride=blocks), :
        ].astype(BF)


def pack_cot_kernel(
    experts, capacity, routes_ref, gates_ref, cot_ref, out_ref, token_ref, wide_ref
):
    masks = slot_masks(routes_ref[...], experts, capacity)
    both = functools.reduce(lambda a, b: a + b, masks)
    gate = functools.reduce(
        lambda a, b: a + b,
        [
            jnp.sum(m * gates_ref[k : k + 1, :], axis=1, keepdims=True)
            for k, m in enumerate(masks)
        ],
    )
    both = both.astype(BF)
    blocks = cot_ref.shape[1] // LANES

    def block(f):
        rows = jnp.dot(
            both, cot_ref[:, f * LANES : (f + 1) * LANES], preferred_element_type=F32
        )
        return rows * gate

    tile_rows(block, blocks, wide_ref, out_ref.at[0])
    out_ref[1] = out_ref[0]
    token_ref[...] = jnp.zeros_like(token_ref)


def pack_input_kernel(experts, capacity, routes_ref, x_ref, after, out_ref, wide_ref):
    masks = slot_masks(routes_ref[...], experts, capacity)
    both = functools.reduce(lambda a, b: a + b, masks).astype(BF)
    blocks = x_ref.shape[0]
    tile_rows(
        lambda f: jnp.dot(both, x_ref[f], preferred_element_type=F32),
        blocks,
        wide_ref,
        out_ref,
    )


def tie_kernel(x_ref, *rest):
    pass


def token_kernel(after, token_ref):
    token_ref[...] = jnp.zeros_like(token_ref)


def split_kernel(x_ref, *outs):
    rows = outs[0].shape[0]
    for i, out_ref in enumerate(outs):
        out_ref[...] = x_ref[i * rows : (i + 1) * rows, :]


def pieces_kernel(c, after, *refs):
    *outs, sems = refs
    flat = c.shape[0] * c.shape[1] // len(outs)
    per = c.shape[1] // flat
    copies = [
        pltpu.make_async_copy(
            c.at[i // per, pl.ds((i % per) * flat, flat)], out_ref, sems.at[i]
        )
        for i, out_ref in enumerate(outs)
    ]
    for copy in copies:
        copy.start()
    for copy in copies:
        copy.wait()


def untile_pieces(pieces, blocks, wide_ref, out_ref):
    at = 0
    for piece in pieces:
        wide_ref[at : at + piece.shape[0], :] = piece[...].astype(F32)
        at += piece.shape[0]
    rows = wide_ref.shape[0] // blocks
    for f in range(blocks):
        out_ref[:, f * LANES : (f + 1) * LANES] = wide_ref[
            pl.ds(f, rows, stride=blocks), :
        ].astype(BF)


def column_block(ref, index, width):
    return ref[:, pl.ds(pl.multiple_of(index * width, LANES), width)]


class Loads:
    def __init__(self, ref, indices, buffer, sems):
        width = buffer.shape[2]
        self.buffer = buffer
        self.copies = [
            pltpu.make_async_copy(
                ref.at[:, pl.ds(pl.multiple_of(index * width, LANES), width)],
                buffer.at[i],
                sems.at[i],
            )
            for i, index in enumerate(indices)
        ]
        for copy in self.copies:
            copy.start()

    def __getitem__(self, i):
        self.copies[i].wait()
        return self.buffer[i]


def dact_first_kernel(place_ref, *refs):
    *c, down, out_ref, wide, lhs = refs
    core = place_ref[0] & 1
    w = [column_block(down, core + 2 * j, lhs.shape[1]) for j in range(2)]
    blocks = lhs.shape[1] // LANES
    half = len(c) // 2
    untile_pieces(c[:half], blocks, wide, lhs)
    out_ref[...] = nt(lhs[...], w[0])
    untile_pieces(c[half:], blocks, wide, lhs)
    out_ref[...] += nt(lhs[...], w[1])


def dact_last_kernel(place_ref, *refs):
    *c, part, down, out_ref, wide, lhs = refs
    core = 1 - (place_ref[0] & 1)
    w = [column_block(down, core + 2 * j, lhs.shape[1]) for j in range(2)]
    blocks = lhs.shape[1] // LANES
    half = len(c) // 2
    untile_pieces(c[:half], blocks, wide, lhs)
    out_ref[...] = part[...] + nt(lhs[...], w[0])
    untile_pieces(c[half:], blocks, wide, lhs)
    out_ref[...] += nt(lhs[...], w[1])


def rows_block(ref, index, width):
    return ref[:, index].reshape(width, -1)


def pre_first_kernel(place_ref, x0, gate, up, g_ref, u_ref, wide, lhs):
    ep = place_ref[0]
    width = lhs.shape[1]
    untile_rows(x0, width // LANES, wide, lhs)
    g_ref[...] = jnp.dot(lhs[...], rows_block(gate, ep, width), preferred_element_type=F32)
    u_ref[...] = jnp.dot(lhs[...], rows_block(up, ep, width), preferred_element_type=F32)


def pre_beside_kernel(place_ref, *refs):
    *x1, g_in, u_in, gate, up, g_ref, u_ref, token_ref, wide, lhs = refs
    ep = place_ref[0] ^ 1
    width = lhs.shape[1]
    untile_pieces(x1, width // LANES, wide, lhs)
    g_ref[...] = g_in[...] + jnp.dot(
        lhs[...], rows_block(gate, ep, width), preferred_element_type=F32
    )
    u_ref[...] = u_in[...] + jnp.dot(
        lhs[...], rows_block(up, ep, width), preferred_element_type=F32
    )
    token_ref[...] = jnp.zeros_like(token_ref)


def pre_next_kernel(place_ref, x2, g_in, u_in, gate, up, g_ref, u_ref, wide, lhs):
    ep = place_ref[0] ^ 2
    width = lhs.shape[1]
    untile_rows(x2, width // LANES, wide, lhs)
    g_ref[...] = g_in[...] + jnp.dot(
        lhs[...], rows_block(gate, ep, width), preferred_element_type=F32
    )
    u_ref[...] = u_in[...] + jnp.dot(
        lhs[...], rows_block(up, ep, width), preferred_element_type=F32
    )


def forward_kernel(
    place_ref, x3, g_in, u_in, gate, up, down,
    act_ref, silu_ref, dsilu_ref, send_ref, wide, lhs,
):
    ep = place_ref[0] ^ 3
    width = lhs.shape[1]
    untile_rows(x3, width // LANES, wide, lhs)
    pre_gate = g_in[...] + jnp.dot(
        lhs[...], rows_block(gate, ep, width), preferred_element_type=F32
    )
    pre_up = u_in[...] + jnp.dot(
        lhs[...], rows_block(up, ep, width), preferred_element_type=F32
    )
    sigmoid = jax.nn.sigmoid(pre_gate)
    silu = pre_gate * sigmoid
    silu_ref[...] = silu
    dsilu_ref[...] = pre_up * sigmoid * (1.0 + pre_gate * (1.0 - sigmoid))
    act_ref[...] = (silu * pre_up).astype(BF)
    send_ref[...] = jnp.dot(
        act_ref[...], column_block(down, ep, width), preferred_element_type=F32
    ).astype(BF)


def keep_kernel(place_ref, act_ref, down, keep_ref):
    keep_ref[...] = jnp.dot(
        act_ref[...],
        column_block(down, place_ref[0] ^ 2, keep_ref.shape[1]),
        preferred_element_type=F32,
    ).astype(BF)


def grad_block(dgate_ref, dup_ref, gate, up, index):
    return nt(dgate_ref[...], gate[index]) + nt(dup_ref[...], up[index])


def grad_kernel(
    place_ref, dact_ref, silu_ref, dsilu_ref, gate, up, dgate_ref, dup_ref, *sends
):
    ep = place_ref[0]
    d_act = dact_ref[...]
    dgate_ref[...] = (d_act * dsilu_ref[...]).astype(BF)
    dup_ref[...] = (d_act * silu_ref[...]).astype(BF)
    send = grad_block(dgate_ref, dup_ref, gate, up, ep ^ 3).astype(BF)
    for i, send_ref in enumerate(sends):
        part = send_ref.shape[1]
        send_ref[...] = send[:, i * part : (i + 1) * part]


def grad_keep_kernel(place_ref, dgate_ref, dup_ref, gate, up, keep_ref):
    keep_ref[...] = grad_block(dgate_ref, dup_ref, gate, up, place_ref[0] ^ 2).astype(BF)


def own_out_kernel(place_ref, act_ref, down, after, send_ref, keep_ref, token_ref):
    token_ref[...] = jnp.zeros_like(token_ref)
    ep = place_ref[0]
    width = send_ref.shape[1]
    send_ref[...] = jnp.dot(
        act_ref[...], column_block(down, ep ^ 1, width), preferred_element_type=F32
    ).astype(BF)
    keep_ref[...] = jnp.dot(
        act_ref[...], column_block(down, ep, width), preferred_element_type=F32
    ).astype(BF)


def own_grad_kernel(place_ref, dgate_ref, dup_ref, gate, up, after, send_ref, keep_ref):
    ep = place_ref[0]
    send_ref[...] = grad_block(dgate_ref, dup_ref, gate, up, ep ^ 1).astype(BF)
    keep_ref[...] = grad_block(dgate_ref, dup_ref, gate, up, ep).astype(BF)


def chip_sum_kernel(keep_ref, came_ref, after, out_ref, token_ref):
    token_ref[...] = jnp.zeros_like(token_ref)
    out_ref[...] = (keep_ref[...].astype(F32) + came_ref[...].astype(F32)).astype(BF)


def finish_out_kernel(keep_ref, near_ref, far_ref, grad_ref, *refs):
    *came, after, out_ref, sum_ref, token_ref, wide_ref, sum_buf, rows_buf, sems = refs
    token_ref[...] = jnp.zeros_like(token_ref)
    for i, ref in enumerate(came):
        cols = slice(i * ref.shape[1], (i + 1) * ref.shape[1])
        sum_buf[:, cols] = (grad_ref[:, cols].astype(F32) + ref[...].astype(F32)).astype(BF)
    sum_copy = pltpu.make_async_copy(sum_buf, sum_ref, sems.at[0])
    sum_copy.start()

    def block(f):
        cols = slice(f * LANES, (f + 1) * LANES)
        parts = [ref[:, cols].astype(F32) for ref in (keep_ref, near_ref, far_ref)]
        return parts[0] + parts[1] + parts[2]

    tile_rows(block, keep_ref.shape[1] // LANES, wide_ref, rows_buf)
    rows_copy = pltpu.make_async_copy(rows_buf, out_ref, sems.at[1])
    rows_copy.start()
    sum_copy.wait()
    rows_copy.wait()


def finish_kernel(keep_ref, near_ref, far_ref, after, out_ref, token_ref, wide_ref):
    token_ref[...] = jnp.zeros_like(token_ref)

    def block(f):
        cols = slice(f * LANES, (f + 1) * LANES)
        parts = [ref[:, cols].astype(F32) for ref in (keep_ref, near_ref, far_ref)]
        return parts[0] + parts[1] + parts[2]

    tile_rows(block, keep_ref.shape[1] // LANES, wide_ref, out_ref)


def combine_out_kernel(
    experts, capacity, routes_ref, gates_ref, cot_ref, rows_ref, out_ref, grad_ref, wide, lhs
):
    masks = slot_masks(routes_ref[...], experts, capacity)
    untile_rows(rows_ref, lhs.shape[1] // LANES, wide, lhs)
    cot = cot_ref[...].astype(F32)
    total = None
    grads = []
    for k, m in enumerate(masks):
        picked = tn(m.astype(BF), lhs[...])
        term = gates_ref[:, k : k + 1] * picked
        total = term if total is None else total + term
        grads.append(jnp.sum(cot * picked, axis=1, keepdims=True))
    out_ref[...] = total.astype(BF)
    grad_ref[...] = jnp.concatenate(grads, axis=1)


def combine_grad_kernel(experts, capacity, routes_ref, rows_ref, out_ref, wide, lhs):
    masks = slot_masks(routes_ref[...], experts, capacity)
    both = functools.reduce(lambda a, b: a + b, masks).astype(BF)
    untile_rows(rows_ref, lhs.shape[1] // LANES, wide, lhs)
    out_ref[...] = tn(both, lhs[...]).astype(BF)


SMEM = pl.BlockSpec(memory_space=pltpu.SMEM)
VMEM = pl.BlockSpec(memory_space=pltpu.VMEM)
ANY = pl.BlockSpec(memory_space=pl.ANY)
HBM = pl.BlockSpec(memory_space=pltpu.HBM)


def call(kernel, specs, outs, scratch, flops, moved, *operands, place_outs=None):
    single = not isinstance(outs, (list, tuple))
    return pl.pallas_call(
        kernel,
        out_shape=outs,
        in_specs=specs,
        out_specs=place_outs or (VMEM if single else [VMEM] * len(outs)),
        scratch_shapes=scratch,
        compiler_params=pltpu.CompilerParams(vmem_limit_bytes=VMEM_BYTES),
        cost_estimate=pl.CostEstimate(flops=flops, bytes_accessed=moved, transcendentals=0),
    )(*operands)


def tie(x, *after):
    return pl.pallas_call(
        tie_kernel,
        out_shape=jax.ShapeDtypeStruct(x.shape, x.dtype),
        in_specs=[ANY] * (1 + len(after)),
        out_specs=ANY,
        input_output_aliases={0: 0},
        compiler_params=pltpu.CompilerParams(vmem_limit_bytes=1024 * 1024),
    )(x, *after)


def local(layer_input, output_cot, routes, gate_values, gate_weight, up_weight, down_weight):
    tokens, picks = routes.shape
    experts = lax.axis_size(("cp", "tp"))
    tp = lax.axis_size("tp")
    ep_size = lax.axis_size("ep")
    capacity = max(2, tokens * picks * 5 // (4 * experts))
    slots = experts * capacity
    width = output_cot.shape[1]
    blocks = width // LANES
    hidden = gate_weight.shape[2]
    tiled = slots * blocks
    place = lax.axis_index("ep").astype(jnp.int32).reshape(1)
    routes_t = routes.T
    gates_t = gate_values.T
    down_w = down_weight[0]
    gate_x = gate_weight.reshape(tp, ep_size, LANES, hidden)
    up_x = up_weight.reshape(tp, ep_size, LANES, hidden)
    gate_q = gate_weight.reshape(ep_size, width, hidden)
    up_q = up_weight.reshape(ep_size, width, hidden)
    shape = jax.ShapeDtypeStruct
    wide = pltpu.VMEM((tiled, LANES), F32)
    lhs = pltpu.VMEM((slots, width), BF)
    near = [(i, i ^ 1) for i in range(ep_size)]
    far = [(i, i ^ 2) for i in range(ep_size)]

    def exchange(rows):
        return lax.all_to_all(
            rows.reshape(experts, capacity * blocks, LANES),
            ("cp", "tp"),
            split_axis=0,
            concat_axis=0,
            tiled=True,
        ).reshape(tiled, LANES)

    moved = slots * width * 6
    dot_flops = 2 * slots * width * hidden
    acc = shape((slots, hidden), F32)
    send_t = shape((slots, width), BF)
    keep_t = shape((slots, width), BF)
    hid = shape((slots, hidden), BF)
    rows_t = shape((tiled, LANES), BF)

    token = shape((8, LANES), F32)
    loads = [pltpu.VMEM((2, hidden, width), BF), pltpu.SemaphoreType.DMA((2,))]

    x_cols = lax.all_to_all(
        layer_input.reshape(tp, tokens, LANES), "tp", split_axis=0, concat_axis=0, tiled=True
    )
    cot_rows, cot_token = call(
        functools.partial(pack_cot_kernel, experts, capacity),
        [VMEM] * 3, [shape((2, tiled, LANES), BF), token], [wide], 10**8, moved,
        routes_t, gates_t, output_cot,
    )
    x_rows = call(
        functools.partial(pack_input_kernel, experts, capacity),
        [VMEM] * 3, rows_t, [wide], 10**8, moved, routes_t, x_cols, cot_token,
    )
    x0 = exchange(x_rows)
    x2 = lax.ppermute(x0, "ep", far)
    chips = experts // tp
    groups = [
        [(z * tp + t) * ep_size + half * 2 + core
         for half in range(2) for z in range(chips) for t in range(tp)]
        for core in range(2)
    ]
    cot_here = lax.all_to_all(
        cot_rows.reshape(2 * experts, capacity * blocks, LANES),
        ("cp", "tp", "ep"), split_axis=0, concat_axis=0, tiled=True, axis_index_groups=groups,
    ).reshape(2, tiled, LANES)
    pre = call(
        pre_first_kernel, [SMEM] + [VMEM] * 3, [acc, acc], [wide, lhs],
        2 * dot_flops, moved, place, x0, gate_x, up_x,
    )
    x1 = call(
        split_kernel, [VMEM], [shape((tiled // RELAY, LANES), BF)] * RELAY, [], 10**6, moved, x0
    )
    x1 = [lax.ppermute(piece, "ep", near) for piece in x1]
    *pre, p_token = call(
        pre_beside_kernel, [SMEM] + [VMEM] * (RELAY + 4), [acc, acc, token], [wide, lhs],
        2 * dot_flops, moved, place, *x1, *pre, gate_x, up_x,
    )
    x2 = tie(x2, p_token)
    x3 = lax.ppermute(x2, "ep", near)
    pre = call(
        pre_next_kernel, [SMEM] + [VMEM] * 3 + [VMEM] * 2, [acc, acc],
        [wide, lhs], 12000000000, moved, place, x2, *pre, gate_x, up_x,
    )
    act, silu, dsilu, out_send = call(
        forward_kernel, [SMEM] + [VMEM] * 3 + [VMEM] * 3, [hid, acc, acc, send_t],
        [wide, lhs],
        3 * dot_flops, moved, place, x3, *pre, gate_x, up_x, down_w,
    )
    out_came = lax.ppermute(out_send, "ep", near)
    out_keep = call(
        keep_kernel, [SMEM, VMEM, VMEM], keep_t, [], dot_flops, moved,
        place, act, down_w,
    )
    out_sum, out_token = call(
        chip_sum_kernel, [VMEM] * 2 + [ANY], [send_t, token], [], 10**6, moved,
        out_keep, out_came, p_token,
    )
    out_far = lax.ppermute(out_sum, "ep", far)
    out_send2, out_keep2, own_token = call(
        own_out_kernel, [SMEM, VMEM, VMEM, ANY], [send_t, keep_t, token], [],
        2 * dot_flops, moved, place, act, down_w, out_token,
    )
    cot_here = call(
        pieces_kernel, [ANY, ANY], [shape((2 * tiled // RELAY, LANES), BF)] * RELAY,
        [pltpu.SemaphoreType.DMA((RELAY,))], 10**6, moved, cot_here, own_token,
        place_outs=[ANY] * RELAY,
    )
    cot_there = [lax.ppermute(piece, "ep", near) for piece in cot_here]
    d_part = call(
        dact_first_kernel, [SMEM] + [VMEM] * (RELAY + 1), acc, [wide, lhs],
        2 * dot_flops, moved, place, *cot_here, down_w,
    )
    far_token = call(token_kernel, [ANY], token, [], LONG, 10**4, out_far)
    d_act = call(
        dact_last_kernel, [SMEM] + [VMEM] * (RELAY + 2), acc, [wide, lhs],
        2 * dot_flops, moved, place, *cot_there, d_part, down_w,
    )
    d_gate, d_up, *grad_sends = call(
        grad_kernel, [SMEM] + [VMEM] * 3 + [VMEM] * 2, [hid, hid] + [shape((slots, width // SUMS), BF)] * SUMS, [],
        4 * dot_flops, moved, place, d_act, silu, dsilu, gate_q, up_q,
    )
    grad_keep = call(
        grad_keep_kernel, [SMEM] + [VMEM] * 4, keep_t, [], 2 * dot_flops, moved,
        place, d_gate, d_up, gate_q, up_q,
    )
    grad_came = [lax.ppermute(send, "ep", near) for send in grad_sends]
    out_near = lax.ppermute(out_send2, "ep", near)
    out_rows, grad_sum, g_token = call(
        finish_out_kernel, [VMEM] * (SUMS + 4) + [ANY], [rows_t, send_t, token],
        [wide, pltpu.VMEM((slots, width), BF), pltpu.VMEM((tiled, LANES), BF),
         pltpu.SemaphoreType.DMA((2,))],
        10**6, 2 * moved, out_keep2, out_near, out_far, grad_keep, *grad_came, far_token,
        place_outs=[ANY, ANY, VMEM],
    )
    grad_far = lax.ppermute(grad_sum, "ep", far)
    grad_send2, grad_keep2 = call(
        own_grad_kernel, [SMEM] + [VMEM] * 4 + [ANY], [send_t, keep_t], [],
        4 * dot_flops, moved, place, d_gate, d_up, gate_q, up_q, g_token,
    )
    grad_near = lax.ppermute(grad_send2, "ep", near)
    out_back = exchange(out_rows)
    last_token = call(token_kernel, [ANY], token, [], LONG, 10**4, grad_far)
    grad_rows, _ = call(
        finish_kernel, [VMEM] * 3 + [ANY], [rows_t, token], [wide], 10**6, moved,
        grad_keep2, grad_near, grad_far, last_token,
    )
    grad_back = exchange(grad_rows)
    moe_output, gate_grad = call(
        functools.partial(combine_out_kernel, experts, capacity), [VMEM] * 4,
        [shape((tokens, width), BF), shape((tokens, picks), F32)], [wide, lhs], 10**8, moved,
        routes_t, gate_values, output_cot, out_back,
    )
    gate_grad = gate_grad + lax.ppermute(gate_grad, "ep", near)
    gate_grad = gate_grad + lax.ppermute(gate_grad, "ep", far)
    input_grad = call(
        functools.partial(combine_grad_kernel, experts, capacity), [VMEM] * 2,
        shape((tokens, width), BF), [wide, lhs], 10**8, moved,
        routes_t, grad_back,
    )
    return (moe_output, input_grad, gate_grad)


def solution(mesh):
    placed = (
        P("cp", ("tp", "ep")),
        P(("cp", "tp"), "ep"),
        P(("cp", "tp"), None),
        P(("cp", "tp"), None),
        P(("cp", "tp"), None, "ep"),
        P(("cp", "tp"), None, "ep"),
        P(("cp", "tp"), "ep", None),
    )
    return jax.shard_map(
        local,
        mesh=mesh,
        in_specs=placed,
        out_specs=(P(("cp", "tp"), "ep"), P(("cp", "tp"), "ep"), P(("cp", "tp"), None)),
        check_vma=False,
    )
```

```python
import functools

import jax
import jax.numpy as jnp
from jax import lax
from jax.experimental import pallas as pl
from jax.experimental.pallas import tpu as pltpu
from jax.sharding import PartitionSpec as P

BF = jnp.bfloat16
F32 = jnp.float32
LANES = 128
VMEM_BYTES = 20 * 1024 * 1024
RELAY = 4
SUMS = 2
LONG = 2 * 10**11


def nt(left, right):
    return lax.dot_general(
        left, right, (((1,), (1,)), ((), ())), preferred_element_type=F32
    )


def tn(left, right):
    return lax.dot_general(
        left, right, (((0,), (0,)), ((), ())), preferred_element_type=F32
    )


def slot_masks(routes, experts, capacity):
    picks, tokens = routes.shape
    expert = lax.broadcasted_iota(jnp.int32, (experts, tokens), 0)
    earlier = (
        lax.broadcasted_iota(jnp.int32, (tokens, tokens), 0)
        < lax.broadcasted_iota(jnp.int32, (tokens, tokens), 1)
    ).astype(F32).astype(BF)
    slot = lax.broadcasted_iota(jnp.int32, (experts * capacity, tokens), 0)
    taken = jnp.zeros((experts, 1), F32)
    masks = []
    for k in range(picks):
        named = routes[k : k + 1, :]
        chosen = (expert == named).astype(F32)
        before = jnp.dot(chosen.astype(BF), earlier, preferred_element_type=F32) + taken
        rank = jnp.sum(before * chosen, axis=0, keepdims=True)
        place = named * capacity + rank.astype(jnp.int32)
        masks.append((slot == place).astype(F32))
        taken = taken + jnp.sum(chosen, axis=1, keepdims=True)
    return masks


def tile_rows(values, blocks, wide_ref, out_ref):
    rows = wide_ref.shape[0] // blocks
    for f in range(blocks):
        wide_ref[pl.ds(f, rows, stride=blocks), :] = values(f)
    out_ref[...] = wide_ref[...].astype(BF)


def untile_rows(in_ref, blocks, wide_ref, out_ref):
    rows = wide_ref.shape[0] // blocks
    wide_ref[...] = in_ref[...].astype(F32)
    for f in range(blocks):
        out_ref[:, f * LANES : (f + 1) * LANES] = wide_ref[
            pl.ds(f, rows, stride=blocks), :
        ].astype(BF)


def pack_cot_kernel(
    experts, capacity, routes_ref, gates_ref, cot_ref, out_ref, token_ref, wide_ref
):
    masks = slot_masks(routes_ref[...], experts, capacity)
    both = functools.reduce(lambda a, b: a + b, masks)
    gate = functools.reduce(
        lambda a, b: a + b,
        [
            jnp.sum(m * gates_ref[k : k + 1, :], axis=1, keepdims=True)
            for k, m in enumerate(masks)
        ],
    )
    both = both.astype(BF)
    blocks = cot_ref.shape[1] // LANES

    def block(f):
        rows = jnp.dot(
            both, cot_ref[:, f * LANES : (f + 1) * LANES], preferred_element_type=F32
        )
        return rows * gate

    tile_rows(block, blocks, wide_ref, out_ref.at[0])
    out_ref[1] = out_ref[0]
    token_ref[...] = jnp.zeros_like(token_ref)


def pack_input_kernel(experts, capacity, routes_ref, x_ref, after, out_ref, wide_ref):
    masks = slot_masks(routes_ref[...], experts, capacity)
    both = functools.reduce(lambda a, b: a + b, masks).astype(BF)
    blocks = x_ref.shape[0]
    tile_rows(
        lambda f: jnp.dot(both, x_ref[f], preferred_element_type=F32),
        blocks,
        wide_ref,
        out_ref,
    )


def tie_kernel(x_ref, *rest):
    pass


def token_kernel(after, token_ref):
    token_ref[...] = jnp.zeros_like(token_ref)


def split_kernel(x_ref, *outs):
    rows = outs[0].shape[0]
    for i, out_ref in enumerate(outs):
        out_ref[...] = x_ref[i * rows : (i + 1) * rows, :]


def pieces_kernel(c, after, *refs):
    *outs, sems = refs
    flat = c.shape[0] * c.shape[1] // len(outs)
    per = c.shape[1] // flat
    copies = [
        pltpu.make_async_copy(
            c.at[i // per, pl.ds((i % per) * flat, flat)], out_ref, sems.at[i]
        )
        for i, out_ref in enumerate(outs)
    ]
    for copy in copies:
        copy.start()
    for copy in copies:
        copy.wait()


def untile_pieces(pieces, blocks, wide_ref, out_ref):
    at = 0
    for piece in pieces:
        wide_ref[at : at + piece.shape[0], :] = piece[...].astype(F32)
        at += piece.shape[0]
    rows = wide_ref.shape[0] // blocks
    for f in range(blocks):
        out_ref[:, f * LANES : (f + 1) * LANES] = wide_ref[
            pl.ds(f, rows, stride=blocks), :
        ].astype(BF)


def column_block(ref, index, width):
    return ref[:, pl.ds(pl.multiple_of(index * width, LANES), width)]


class Loads:
    def __init__(self, ref, indices, buffer, sems):
        width = buffer.shape[2]
        self.buffer = buffer
        self.copies = [
            pltpu.make_async_copy(
                ref.at[:, pl.ds(pl.multiple_of(index * width, LANES), width)],
                buffer.at[i],
                sems.at[i],
            )
            for i, index in enumerate(indices)
        ]
        for copy in self.copies:
            copy.start()

    def __getitem__(self, i):
        self.copies[i].wait()
        return self.buffer[i]


def dact_first_kernel(place_ref, *refs):
    *c, down, out_ref, wide, lhs = refs
    core = place_ref[0] & 1
    w = [column_block(down, core + 2 * j, lhs.shape[1]) for j in range(2)]
    blocks = lhs.shape[1] // LANES
    half = len(c) // 2
    untile_pieces(c[:half], blocks, wide, lhs)
    out_ref[...] = nt(lhs[...], w[0])
    untile_pieces(c[half:], blocks, wide, lhs)
    out_ref[...] += nt(lhs[...], w[1])


def dact_last_kernel(place_ref, *refs):
    *c, part, down, out_ref, wide, lhs = refs
    core = 1 - (place_ref[0] & 1)
    w = [column_block(down, core + 2 * j, lhs.shape[1]) for j in range(2)]
    blocks = lhs.shape[1] // LANES
    half = len(c) // 2
    untile_pieces(c[:half], blocks, wide, lhs)
    out_ref[...] = part[...] + nt(lhs[...], w[0])
    untile_pieces(c[half:], blocks, wide, lhs)
    out_ref[...] += nt(lhs[...], w[1])


def rows_block(ref, index, width):
    return ref[:, index].reshape(width, -1)


def pre_first_kernel(place_ref, x0, gate, up, g_ref, u_ref, wide, lhs):
    ep = place_ref[0]
    width = lhs.shape[1]
    untile_rows(x0, width // LANES, wide, lhs)
    g_ref[...] = jnp.dot(lhs[...], rows_block(gate, ep, width), preferred_element_type=F32)
    u_ref[...] = jnp.dot(lhs[...], rows_block(up, ep, width), preferred_element_type=F32)


def pre_beside_kernel(place_ref, *refs):
    *x1, g_in, u_in, gate, up, g_ref, u_ref, token_ref, wide, lhs = refs
    ep = place_ref[0] ^ 1
    width = lhs.shape[1]
    untile_pieces(x1, width // LANES, wide, lhs)
    g_ref[...] = g_in[...] + jnp.dot(
        lhs[...], rows_block(gate, ep, width), preferred_element_type=F32
    )
    u_ref[...] = u_in[...] + jnp.dot(
        lhs[...], rows_block(up, ep, width), preferred_element_type=F32
    )
    token_ref[...] = jnp.zeros_like(token_ref)


def pre_next_kernel(place_ref, x2, g_in, u_in, gate, up, g_ref, u_ref, wide, lhs):
    ep = place_ref[0] ^ 2
    width = lhs.shape[1]
    untile_rows(x2, width // LANES, wide, lhs)
    g_ref[...] = g_in[...] + jnp.dot(
        lhs[...], rows_block(gate, ep, width), preferred_element_type=F32
    )
    u_ref[...] = u_in[...] + jnp.dot(
        lhs[...], rows_block(up, ep, width), preferred_element_type=F32
    )


def forward_kernel(
    place_ref, x3, g_in, u_in, gate, up, down,
    act_ref, silu_ref, dsilu_ref, send_ref, wide, lhs,
):
    ep = place_ref[0] ^ 3
    width = lhs.shape[1]
    untile_rows(x3, width // LANES, wide, lhs)
    pre_gate = g_in[...] + jnp.dot(
        lhs[...], rows_block(gate, ep, width), preferred_element_type=F32
    )
    pre_up = u_in[...] + jnp.dot(
        lhs[...], rows_block(up, ep, width), preferred_element_type=F32
    )
    sigmoid = jax.nn.sigmoid(pre_gate)
    silu = pre_gate * sigmoid
    silu_ref[...] = silu
    dsilu_ref[...] = pre_up * sigmoid * (1.0 + pre_gate * (1.0 - sigmoid))
    act_ref[...] = (silu * pre_up).astype(BF)
    send_ref[...] = jnp.dot(
        act_ref[...], column_block(down, ep, width), preferred_element_type=F32
    ).astype(BF)


def keep_kernel(place_ref, act_ref, down, keep_ref):
    keep_ref[...] = jnp.dot(
        act_ref[...],
        column_block(down, place_ref[0] ^ 2, keep_ref.shape[1]),
        preferred_element_type=F32,
    ).astype(BF)


def grad_block(dgate_ref, dup_ref, gate, up, index):
    return nt(dgate_ref[...], gate[index]) + nt(dup_ref[...], up[index])


def grad_kernel(
    place_ref, dact_ref, silu_ref, dsilu_ref, gate, up, dgate_ref, dup_ref, *sends
):
    ep = place_ref[0]
    d_act = dact_ref[...]
    dgate_ref[...] = (d_act * dsilu_ref[...]).astype(BF)
    dup_ref[...] = (d_act * silu_ref[...]).astype(BF)
    send = grad_block(dgate_ref, dup_ref, gate, up, ep ^ 3).astype(BF)
    for i, send_ref in enumerate(sends):
        part = send_ref.shape[1]
        send_ref[...] = send[:, i * part : (i + 1) * part]


def grad_keep_kernel(place_ref, dgate_ref, dup_ref, gate, up, keep_ref):
    keep_ref[...] = grad_block(dgate_ref, dup_ref, gate, up, place_ref[0] ^ 2).astype(BF)


def own_out_kernel(place_ref, act_ref, down, after, keep_ref, token_ref, *sends):
    token_ref[...] = jnp.zeros_like(token_ref)
    ep = place_ref[0]
    width = keep_ref.shape[1]
    send = jnp.dot(
        act_ref[...], column_block(down, ep ^ 1, width), preferred_element_type=F32
    ).astype(BF)
    for i, send_ref in enumerate(sends):
        part = send_ref.shape[1]
        send_ref[...] = send[:, i * part : (i + 1) * part]
    keep_ref[...] = jnp.dot(
        act_ref[...], column_block(down, ep, width), preferred_element_type=F32
    ).astype(BF)


def own_grad_kernel(place_ref, dgate_ref, dup_ref, gate, up, after, send_ref, keep_ref):
    ep = place_ref[0]
    send_ref[...] = grad_block(dgate_ref, dup_ref, gate, up, ep ^ 1).astype(BF)
    keep_ref[...] = grad_block(dgate_ref, dup_ref, gate, up, ep).astype(BF)


def chip_sum_kernel(keep_ref, came_ref, after, out_ref, token_ref):
    token_ref[...] = jnp.zeros_like(token_ref)
    out_ref[...] = (keep_ref[...].astype(F32) + came_ref[...].astype(F32)).astype(BF)


def finish_out_kernel(pieces, keep_ref, far_ref, grad_ref, *refs):
    near, refs = refs[:pieces], refs[pieces:]
    *came, after, out_ref, sum_ref, token_ref, wide_ref, sum_buf, rows_buf, sems = refs
    token_ref[...] = jnp.zeros_like(token_ref)
    for i, ref in enumerate(came):
        cols = slice(i * ref.shape[1], (i + 1) * ref.shape[1])
        sum_buf[:, cols] = (grad_ref[:, cols].astype(F32) + ref[...].astype(F32)).astype(BF)
    sum_copy = pltpu.make_async_copy(sum_buf, sum_ref, sems.at[0])
    sum_copy.start()

    def block(f):
        cols = slice(f * LANES, (f + 1) * LANES)
        at = f * LANES % near[0].shape[1]
        beside = near[f * LANES // near[0].shape[1]][:, at : at + LANES]
        parts = [part.astype(F32) for part in (keep_ref[:, cols], beside, far_ref[:, cols])]
        return parts[0] + parts[1] + parts[2]

    tile_rows(block, keep_ref.shape[1] // LANES, wide_ref, rows_buf)
    rows_copy = pltpu.make_async_copy(rows_buf, out_ref, sems.at[1])
    rows_copy.start()
    sum_copy.wait()
    rows_copy.wait()


def finish_kernel(keep_ref, near_ref, far_ref, after, out_ref, token_ref, wide_ref):
    token_ref[...] = jnp.zeros_like(token_ref)

    def block(f):
        cols = slice(f * LANES, (f + 1) * LANES)
        parts = [ref[:, cols].astype(F32) for ref in (keep_ref, near_ref, far_ref)]
        return parts[0] + parts[1] + parts[2]

    tile_rows(block, keep_ref.shape[1] // LANES, wide_ref, out_ref)


def combine_out_kernel(
    experts, capacity, routes_ref, gates_ref, cot_ref, rows_ref, out_ref, grad_ref, wide, lhs
):
    masks = slot_masks(routes_ref[...], experts, capacity)
    untile_rows(rows_ref, lhs.shape[1] // LANES, wide, lhs)
    cot = cot_ref[...].astype(F32)
    total = None
    grads = []
    for k, m in enumerate(masks):
        picked = tn(m.astype(BF), lhs[...])
        term = gates_ref[:, k : k + 1] * picked
        total = term if total is None else total + term
        grads.append(jnp.sum(cot * picked, axis=1, keepdims=True))
    out_ref[...] = total.astype(BF)
    grad_ref[...] = jnp.concatenate(grads, axis=1)


def combine_grad_kernel(experts, capacity, routes_ref, rows_ref, out_ref, wide, lhs):
    masks = slot_masks(routes_ref[...], experts, capacity)
    both = functools.reduce(lambda a, b: a + b, masks).astype(BF)
    untile_rows(rows_ref, lhs.shape[1] // LANES, wide, lhs)
    out_ref[...] = tn(both, lhs[...]).astype(BF)


SMEM = pl.BlockSpec(memory_space=pltpu.SMEM)
VMEM = pl.BlockSpec(memory_space=pltpu.VMEM)
ANY = pl.BlockSpec(memory_space=pl.ANY)
HBM = pl.BlockSpec(memory_space=pltpu.HBM)


def call(kernel, specs, outs, scratch, flops, moved, *operands, place_outs=None):
    single = not isinstance(outs, (list, tuple))
    return pl.pallas_call(
        kernel,
        out_shape=outs,
        in_specs=specs,
        out_specs=place_outs or (VMEM if single else [VMEM] * len(outs)),
        scratch_shapes=scratch,
        compiler_params=pltpu.CompilerParams(vmem_limit_bytes=VMEM_BYTES),
        cost_estimate=pl.CostEstimate(flops=flops, bytes_accessed=moved, transcendentals=0),
    )(*operands)


def tie(x, *after):
    return pl.pallas_call(
        tie_kernel,
        out_shape=jax.ShapeDtypeStruct(x.shape, x.dtype),
        in_specs=[ANY] * (1 + len(after)),
        out_specs=ANY,
        input_output_aliases={0: 0},
        compiler_params=pltpu.CompilerParams(vmem_limit_bytes=1024 * 1024),
    )(x, *after)


def local(layer_input, output_cot, routes, gate_values, gate_weight, up_weight, down_weight):
    tokens, picks = routes.shape
    experts = lax.axis_size(("cp", "tp"))
    tp = lax.axis_size("tp")
    ep_size = lax.axis_size("ep")
    capacity = max(2, tokens * picks * 5 // (4 * experts))
    slots = experts * capacity
    width = output_cot.shape[1]
    blocks = width // LANES
    hidden = gate_weight.shape[2]
    tiled = slots * blocks
    place = lax.axis_index("ep").astype(jnp.int32).reshape(1)
    routes_t = routes.T
    gates_t = gate_values.T
    down_w = down_weight[0]
    gate_x = gate_weight.reshape(tp, ep_size, LANES, hidden)
    up_x = up_weight.reshape(tp, ep_size, LANES, hidden)
    gate_q = gate_weight.reshape(ep_size, width, hidden)
    up_q = up_weight.reshape(ep_size, width, hidden)
    shape = jax.ShapeDtypeStruct
    wide = pltpu.VMEM((tiled, LANES), F32)
    lhs = pltpu.VMEM((slots, width), BF)
    near = [(i, i ^ 1) for i in range(ep_size)]
    far = [(i, i ^ 2) for i in range(ep_size)]

    def exchange(rows):
        return lax.all_to_all(
            rows.reshape(experts, capacity * blocks, LANES),
            ("cp", "tp"),
            split_axis=0,
            concat_axis=0,
            tiled=True,
        ).reshape(tiled, LANES)

    moved = slots * width * 6
    dot_flops = 2 * slots * width * hidden
    acc = shape((slots, hidden), F32)
    send_t = shape((slots, width), BF)
    keep_t = shape((slots, width), BF)
    hid = shape((slots, hidden), BF)
    rows_t = shape((tiled, LANES), BF)

    token = shape((8, LANES), F32)
    loads = [pltpu.VMEM((2, hidden, width), BF), pltpu.SemaphoreType.DMA((2,))]

    x_cols = lax.all_to_all(
        layer_input.reshape(tp, tokens, LANES), "tp", split_axis=0, concat_axis=0, tiled=True
    )
    cot_rows, cot_token = call(
        functools.partial(pack_cot_kernel, experts, capacity),
        [VMEM] * 3, [shape((2, tiled, LANES), BF), token], [wide], 10**8, moved,
        routes_t, gates_t, output_cot,
    )
    x_rows = call(
        functools.partial(pack_input_kernel, experts, capacity),
        [VMEM] * 3, rows_t, [wide], 10**8, moved, routes_t, x_cols, cot_token,
    )
    x0 = exchange(x_rows)
    x2 = lax.ppermute(x0, "ep", far)
    chips = experts // tp
    groups = [
        [(z * tp + t) * ep_size + half * 2 + core
         for half in range(2) for z in range(chips) for t in range(tp)]
        for core in range(2)
    ]
    cot_here = lax.all_to_all(
        cot_rows.reshape(2 * experts, capacity * blocks, LANES),
        ("cp", "tp", "ep"), split_axis=0, concat_axis=0, tiled=True, axis_index_groups=groups,
    ).reshape(2, tiled, LANES)
    pre = call(
        pre_first_kernel, [SMEM] + [VMEM] * 3, [acc, acc], [wide, lhs],
        2 * dot_flops, moved, place, x0, gate_x, up_x,
    )
    x1 = call(
        split_kernel, [VMEM], [shape((tiled // RELAY, LANES), BF)] * RELAY, [], 10**6, moved, x0
    )
    x1 = [lax.ppermute(piece, "ep", near) for piece in x1]
    *pre, p_token = call(
        pre_beside_kernel, [SMEM] + [VMEM] * (RELAY + 4), [acc, acc, token], [wide, lhs],
        2 * dot_flops, moved, place, *x1, *pre, gate_x, up_x,
    )
    x2 = tie(x2, p_token)
    x3 = lax.ppermute(x2, "ep", near)
    pre = call(
        pre_next_kernel, [SMEM] + [VMEM] * 3 + [VMEM] * 2, [acc, acc],
        [wide, lhs], 12000000000, moved, place, x2, *pre, gate_x, up_x,
    )
    act, silu, dsilu, out_send = call(
        forward_kernel, [SMEM] + [VMEM] * 3 + [VMEM] * 3, [hid, acc, acc, send_t],
        [wide, lhs],
        3 * dot_flops, moved, place, x3, *pre, gate_x, up_x, down_w,
    )
    out_came = lax.ppermute(out_send, "ep", near)
    out_keep = call(
        keep_kernel, [SMEM, VMEM, VMEM], keep_t, [], dot_flops, moved,
        place, act, down_w,
    )
    out_sum, out_token = call(
        chip_sum_kernel, [VMEM] * 2 + [ANY], [send_t, token], [], 10**6, moved,
        out_keep, out_came, p_token,
    )
    out_far = lax.ppermute(out_sum, "ep", far)
    out_keep2, own_token, *out_sends2 = call(
        own_out_kernel, [SMEM, VMEM, VMEM, ANY],
        [keep_t, token] + [shape((slots, width // SUMS), BF)] * SUMS, [],
        2 * dot_flops, moved, place, act, down_w, out_token,
    )
    cot_here = call(
        pieces_kernel, [ANY, ANY], [shape((2 * tiled // RELAY, LANES), BF)] * RELAY,
        [pltpu.SemaphoreType.DMA((RELAY,))], 10**6, moved, cot_here, own_token,
        place_outs=[ANY] * RELAY,
    )
    cot_there = [lax.ppermute(piece, "ep", near) for piece in cot_here]
    d_part = call(
        dact_first_kernel, [SMEM] + [VMEM] * (RELAY + 1), acc, [wide, lhs],
        2 * dot_flops, moved, place, *cot_here, down_w,
    )
    far_token = call(token_kernel, [ANY], token, [], LONG, 10**4, out_far)
    d_act = call(
        dact_last_kernel, [SMEM] + [VMEM] * (RELAY + 2), acc, [wide, lhs],
        2 * dot_flops, moved, place, *cot_there, d_part, down_w,
    )
    d_gate, d_up, *grad_sends = call(
        grad_kernel, [SMEM] + [VMEM] * 3 + [VMEM] * 2, [hid, hid] + [shape((slots, width // SUMS), BF)] * SUMS, [],
        4 * dot_flops, moved, place, d_act, silu, dsilu, gate_q, up_q,
    )
    grad_keep = call(
        grad_keep_kernel, [SMEM] + [VMEM] * 4, keep_t, [], 2 * dot_flops, moved,
        place, d_gate, d_up, gate_q, up_q,
    )
    grad_came = [lax.ppermute(send, "ep", near) for send in grad_sends]
    out_near = [lax.ppermute(send, "ep", near) for send in out_sends2]
    out_rows, grad_sum, g_token = call(
        functools.partial(finish_out_kernel, SUMS), [VMEM] * (2 * SUMS + 3) + [ANY],
        [rows_t, send_t, token],
        [wide, pltpu.VMEM((slots, width), BF), pltpu.VMEM((tiled, LANES), BF),
         pltpu.SemaphoreType.DMA((2,))],
        10**6, 2 * moved, out_keep2, out_far, grad_keep, *out_near, *grad_came, far_token,
        place_outs=[ANY, ANY, VMEM],
    )
    grad_far = lax.ppermute(grad_sum, "ep", far)
    grad_send2, grad_keep2 = call(
        own_grad_kernel, [SMEM] + [VMEM] * 4 + [ANY], [send_t, keep_t], [],
        4 * dot_flops, moved, place, d_gate, d_up, gate_q, up_q, g_token,
    )
    grad_near = lax.ppermute(grad_send2, "ep", near)
    out_back = exchange(out_rows)
    last_token = call(token_kernel, [ANY], token, [], LONG, 10**4, grad_far)
    grad_rows, _ = call(
        finish_kernel, [VMEM] * 3 + [ANY], [rows_t, token], [wide], 10**6, moved,
        grad_keep2, grad_near, grad_far, last_token,
    )
    grad_back = exchange(grad_rows)
    moe_output, gate_grad = call(
        functools.partial(combine_out_kernel, experts, capacity), [VMEM] * 4,
        [shape((tokens, width), BF), shape((tokens, picks), F32)], [wide, lhs], 10**8, moved,
        routes_t, gate_values, output_cot, out_back,
    )
    gate_grad = gate_grad + lax.ppermute(gate_grad, "ep", near)
    gate_grad = gate_grad + lax.ppermute(gate_grad, "ep", far)
    input_grad = call(
        functools.partial(combine_grad_kernel, experts, capacity), [VMEM] * 2,
        shape((tokens, width), BF), [wide, lhs], 10**8, moved,
        routes_t, grad_back,
    )
    return (moe_output, input_grad, gate_grad)


def solution(mesh):
    placed = (
        P("cp", ("tp", "ep")),
        P(("cp", "tp"), "ep"),
        P(("cp", "tp"), None),
        P(("cp", "tp"), None),
        P(("cp", "tp"), None, "ep"),
        P(("cp", "tp"), None, "ep"),
        P(("cp", "tp"), "ep", None),
    )
    return jax.shard_map(
        local,
        mesh=mesh,
        in_specs=placed,
        out_specs=(P(("cp", "tp"), "ep"), P(("cp", "tp"), "ep"), P(("cp", "tp"), None)),
        check_vma=False,
    )
```
